256 devices in a mesh: row: 8 (over x, z_hi), col: 32 (over z_lo, y, core).
Axes of the slice: x: 4, y: 4, z: 8 (z_hi: 2, z_lo: 4; z = z_hi * 4 + z_lo), core: 2. Of those that a mesh axis runs over, the one named last changes fastest.
Arguments:
- src_feat: bfloat16 [131072, 128], P('col'), may hold values from -68 to 68
- dst_feat: bfloat16 [16384, 128], P(('row', 'col')), may hold values from -6 to 6
- weight: bfloat16 [128, 512], replicated, may hold values from -0.5 to 0.5
- att_src: float32 [8, 64], replicated, may hold values from -4 to 4
- att_dst: float32 [8, 64], replicated, may hold values from -4 to 4
- bias: float32 [512], replicated, may hold values from -3 to 3
- tile_rows: int32 [8, 32, 160], P('row', 'col'), may hold values from 0 to 15
- tile_cols: int32 [8, 32, 160], P('row', 'col'), may hold values from 0 to 31
- tile_masks: int32 [8, 32, 160, 128, 128], P('row', 'col'), may hold values 0 or 1
- tile_count: int32 [8, 32], P('row', 'col'), may hold values from 40 to 160, as said below
Outputs:
- node_out: float32 [16384, 512], P(('row', 'col'))
The draws below stay inside these ranges and needn't reach their ends.
Inputs may be any that keep to these rules, and one draw needn't show every extreme that they name: Device (r, c) uses its first tile_count[r, c] tile slots; later slots hold arbitrary entries that are not part of the graph; some device uses all 160 slots.
All inputs are finite; a program needn't handle non-finite values. No bound on the sum of `tile_masks` on one device may be relied on, other than what follows from the above.
Results may differ from the reference program's by a relative error of at most 0.0042.
Values may be sent and summed in bfloat16 or wider, within the bound.
A program may use at most 128 MiB of HBM per device.

```python
import jax
import jax.numpy as jnp
from jax import lax

FIN = 128
HEADS = 8
HEAD_DIM = 64
TILE = 128
D_ROW = 2048
S_COL = 4096
TILES = 160
NDST = 16384
NSRC = 131072
FEAT = 512
N_ROW = 8
N_COL = 32


def draw_src_feat(key, part):
    key = jax.random.fold_in(key, 11)
    first = jax.random.fold_in(key, 0)
    return jax.random.truncated_normal(first, -6.0, 6.0, (NSRC, FIN), jnp.float32).astype(jnp.bfloat16)


def draw_tile_count(key, part):
    key = jax.random.fold_in(key, 5)
    first, second = jax.random.split(key)
    level = jax.random.randint(first, (N_ROW, N_COL), 0, 64)
    lowest = TILES // 4
    counts = lowest + (TILES - lowest) * level * level // (63 * 63)
    chosen = jax.random.randint(second, (), 0, N_ROW * N_COL)
    flat = counts.reshape(-1)
    flat = jnp.where(jnp.arange(N_ROW * N_COL) == chosen, TILES, flat)
    return flat.reshape(N_ROW, N_COL).astype(jnp.int32)


def touch_ends(array, key, low, largest):
    index_at = [jax.random.randint(jax.random.fold_in(key, axis), (), 0, length) for axis, length in enumerate(array.shape)]
    main_axis = array.shape.index(max(array.shape))
    next_to = index_at[:main_axis] + [(index_at[main_axis] + 1) % array.shape[main_axis]] + index_at[main_axis + 1:]
    return array.at[tuple(index_at)].set(low).at[tuple(next_to)].set(largest)


def shard_levels(rng, dims, cuts, smallest, top_value):
    level = 1.0
    for axis_at, parts in cuts:
        draws = jax.random.uniform(jax.random.fold_in(jax.random.fold_in(rng, 6), axis_at), (parts,), jnp.float32, smallest / len(cuts), top_value / len(cuts))
        level = level * jnp.repeat(jnp.exp(draws), dims[axis_at] // parts).reshape((-1,) + (1,) * (len(dims) - 1 - axis_at))
    return level


def normal_values(stream_key, dims, deviation, limit, shards=(), dtype=jnp.bfloat16):
    drawn = deviation * jax.random.normal(stream_key, dims, jnp.float32)
    if shards:
        drawn = drawn * shard_levels(stream_key, dims, shards, -0.22, 0.18)
    return jnp.clip(drawn, -limit, limit).astype(dtype)


def setup_inputs(seed: int = 0) -> dict:
    key_of = jax.random.split(jax.random.key(seed), 11)
    src_feat = draw_src_feat(jax.random.fold_in(key_of[10], 71), 0)
    dst_feat = normal_values(key_of[1], (NDST, FIN), 1.0, 6.0, ((0, 256),))
    weight = normal_values(key_of[2], (FIN, FEAT), FIN ** -0.5, 0.5)
    att_src = normal_values(key_of[3], (HEADS, HEAD_DIM), 0.3, 4.0, (), jnp.float32)
    att_dst = normal_values(key_of[4], (HEADS, HEAD_DIM), 0.3, 4.0, (), jnp.float32)
    bias = normal_values(key_of[5], (FEAT,), 0.5, 3.0, (), jnp.float32)
    tile_rows = touch_ends(jax.random.randint(key_of[6], (N_ROW, N_COL, TILES), 0, D_ROW // TILE), jax.random.fold_in(key_of[6], 1), 0, (D_ROW // TILE) - 1).astype(jnp.int32)
    tile_cols = touch_ends(jax.random.randint(key_of[7], (N_ROW, N_COL, TILES), 0, S_COL // TILE), jax.random.fold_in(key_of[7], 1), 0, (S_COL // TILE) - 1).astype(jnp.int32)
    tile_masks = touch_ends((jax.random.randint(key_of[8], (N_ROW, N_COL, TILES, TILE, TILE), 0, 16) < 1).astype(jnp.int32), jax.random.fold_in(key_of[8], 1), 0, 1)
    tile_count = draw_tile_count(jax.random.fold_in(key_of[10], 71), 0)
    return dict(src_feat=src_feat, dst_feat=dst_feat, weight=weight, att_src=att_src, att_dst=att_dst, bias=bias, tile_rows=tile_rows, tile_cols=tile_cols, tile_masks=tile_masks, tile_count=tile_count)


NEG_FILL = -1.0e30


def leaky_relu(values):
    return jnp.where(values > 0, values, 0.2 * values)


def project_rows(features, weight):
    values = jnp.dot(features, weight, preferred_element_type=jnp.float32).astype(jnp.bfloat16)
    return lax.optimization_barrier(values)


def head_scores(values, attention):
    row_count = values.shape[0]
    wide = values.astype(jnp.float32).reshape(row_count, HEADS, HEAD_DIM)
    return jnp.sum(wide * attention[None], axis=2)


def tile_update(carry_state, dst_scores, src_scores, src_values, tile_mask, row_start, col_start):
    run_max, run_sum, run_acc = carry_state
    dst_part = lax.dynamic_slice_in_dim(dst_scores, row_start, TILE, 1)
    src_part = lax.dynamic_slice_in_dim(src_scores, col_start, TILE, 1)
    logits = leaky_relu(dst_part[:, :, None] + src_part[:, None, :])
    present = tile_mask[None] > 0
    logits = jnp.where(present, logits, NEG_FILL)
    old_max = lax.dynamic_slice_in_dim(run_max, row_start, TILE, 1)
    new_max = jnp.maximum(old_max, jnp.max(logits, axis=2))
    probs = jnp.where(present, jnp.exp(logits - new_max[:, :, None]), 0.0)
    keep_old = jnp.exp(old_max - new_max)
    old_sum = lax.dynamic_slice_in_dim(run_sum, row_start, TILE, 1)
    new_sum = old_sum * keep_old + jnp.sum(probs, axis=2)
    rounded = lax.optimization_barrier(probs.astype(jnp.bfloat16)).astype(jnp.float32)
    block_vals = lax.dynamic_slice_in_dim(src_values, col_start, TILE, 0).astype(jnp.float32)
    block_vals = block_vals.reshape(TILE, HEADS, HEAD_DIM)
    message = jnp.einsum("hij,jhc->ihc", rounded, block_vals, precision=lax.Precision.HIGHEST)
    old_acc = lax.dynamic_slice_in_dim(run_acc, row_start, TILE, 0).reshape(TILE, HEADS, HEAD_DIM)
    new_acc = (old_acc * keep_old.T[:, :, None] + message).reshape(TILE, HEADS * HEAD_DIM)
    run_max = lax.dynamic_update_slice_in_dim(run_max, new_max, row_start, 1)
    run_sum = lax.dynamic_update_slice_in_dim(run_sum, new_sum, row_start, 1)
    run_acc = lax.dynamic_update_slice_in_dim(run_acc, new_acc, row_start, 0)
    return (run_max, run_sum, run_acc)


def finish(row_top, row_sums, row_acc, self_logit, own_values, bias):
    last_max = jnp.maximum(row_top, self_logit)
    keep_old = jnp.exp(row_top - last_max)
    keep_self = jnp.exp(self_logit - last_max)
    denominator = row_sums * keep_old + keep_self
    row_count = row_acc.shape[0]
    own_wide = own_values.astype(jnp.float32).reshape(row_count, HEADS, HEAD_DIM)
    combined = row_acc.reshape(row_count, HEADS, HEAD_DIM) * keep_old[:, :, None] + keep_self[:, :, None] * own_wide
    mixed = (combined / denominator[:, :, None]).reshape(row_count, HEADS * HEAD_DIM)
    return jax.nn.elu(mixed + bias[None]).astype(jnp.float32)


def reference(src_feat, dst_feat, weight, att_src, att_dst, bias, tile_rows, tile_cols, tile_masks, tile_count):
    src_values = project_rows(src_feat, weight)
    dst_values = project_rows(dst_feat, weight)
    src_scores = head_scores(src_values, att_src).T
    dst_own = head_scores(dst_values, att_dst)
    dst_cross = head_scores(dst_values, att_src)
    dst_scores = dst_own.T
    run_max = jnp.full((HEADS, NDST), NEG_FILL, jnp.float32)
    run_sum = jnp.zeros((HEADS, NDST), jnp.float32)
    run_acc = jnp.zeros((NDST, HEADS * HEAD_DIM), jnp.float32)

    def device_pass(device, carry_state):
        device = device.astype(jnp.int32)
        row_idx = (device // N_COL).astype(jnp.int32)
        col_idx = (device % N_COL).astype(jnp.int32)

        def one_tile(tile_slot, inner_state):
            tile_slot = tile_slot.astype(jnp.int32)
            row_start = (row_idx * D_ROW + tile_rows[row_idx, col_idx, tile_slot] * TILE).astype(jnp.int32)
            col_start = (col_idx * S_COL + tile_cols[row_idx, col_idx, tile_slot] * TILE).astype(jnp.int32)
            return tile_update(inner_state, dst_scores, src_scores, src_values,
                               tile_masks[row_idx, col_idx, tile_slot], row_start, col_start)

        return lax.fori_loop(jnp.int32(0), tile_count[row_idx, col_idx].astype(jnp.int32), one_tile, carry_state)

    run_max, run_sum, run_acc = lax.fori_loop(jnp.int32(0), jnp.int32(N_ROW * N_COL), device_pass,
                                              (run_max, run_sum, run_acc))
    self_logit = leaky_relu(dst_own + dst_cross)
    return finish(run_max.T, run_sum.T, run_acc, self_logit, dst_values, bias)
```

```python
import functools

import jax
import jax.numpy as jnp
from jax import lax
from jax.experimental import pallas as pl
from jax.experimental.pallas import tpu as pltpu
from jax.sharding import PartitionSpec as P

HEADS = 8
HEAD_DIM = 64
TILE = 128
FEAT = HEADS * HEAD_DIM
NEG = -1e30
SPAN = 50.0
HALF = FEAT // 2
HALF_HEADS = HEADS // 2
BLOCK = HALF + 16
AUG = HEAD_DIM + 16
RING = 12
ORDER = 256

f32 = jnp.float32
bf16 = jnp.bfloat16


def leaky_relu(values):
    return jnp.maximum(values, 0.2 * values)


def split3(values):
    high = values.astype(bf16)
    rest = values - high.astype(f32)
    middle = rest.astype(bf16)
    low = (rest - middle.astype(f32)).astype(bf16)
    return high, middle, low


def transposed_dot(left, right):
    return lax.dot_general(left, right, (((0,), (0,)), ((), ())), preferred_element_type=f32)


def project_t(weight, features):
    return lax.dot_general(weight, features, (((0,), (1,)), ((), ())), preferred_element_type=f32).astype(bf16)


def attention_column(attention):
    wide = jnp.concatenate([attention] * HEADS, axis=1)
    head = lax.broadcasted_iota(jnp.int32, wide.shape, 0)
    lane_head = lax.broadcasted_iota(jnp.int32, wide.shape, 1) // HEAD_DIM
    wide = jnp.where(head == lane_head, wide, 0.0)
    terms = jnp.concatenate([part.astype(f32) for part in split3(wide)], axis=0).astype(bf16)
    return transposed_dot(terms, jnp.ones((terms.shape[0], 128), bf16))


def head_rows(values, column):
    product = values * column
    return [
        jnp.sum(product[h * HEAD_DIM : (h + 1) * HEAD_DIM], axis=0, keepdims=True) for h in range(HEADS)
    ]


def as_column(row, rows):
    return jnp.transpose(jnp.broadcast_to(row, (rows, row.shape[1])))


def scores_kernel(n_col, dst_ref, weight_ref, att_ref, rows_ref, cols_ref, count_ref,
                  score_ref, chip_ref, order_ref, pairs_ref, own, send_sem, recv_sem, feat_send, feat_recv):
    me = lax.axis_index("col")
    core = lax.rem(me, 2)
    partner = me + 1 - 2 * core
    barrier = pltpu.get_barrier_semaphore()

    def greet(step, carry):
        pl.semaphore_signal(barrier, inc=1, device_id={"col": lax.rem(me + step, n_col)},
                            device_id_type=pl.DeviceIdType.MESH)
        return carry

    lax.fori_loop(1, n_col, greet, 0)

    features = dst_ref[...]
    both = jnp.concatenate([features, features], axis=0)
    side = lax.broadcasted_iota(jnp.int32, both.shape, 0) // features.shape[0]
    both = jnp.where(side == core, both, jnp.zeros_like(both))
    values = project_t(weight_ref[...], both).astype(f32)
    own[...] = jnp.concatenate(head_rows(values, attention_column(att_ref[...])), axis=0)
    score_ref[me] = own[...]
    half = features.shape[0]
    chip_ref[pl.ds(pl.multiple_of(core * half, half), half), :] = features

    pl.semaphore_wait(barrier, n_col - 1)

    def score_copy(target, source_slot):
        return pltpu.make_async_remote_copy(
            src_ref=own, dst_ref=score_ref.at[me], send_sem=send_sem.at[target], recv_sem=recv_sem.at[source_slot],
            device_id={"col": target}, device_id_type=pl.DeviceIdType.MESH)

    def send(step, carry):
        score_copy(lax.rem(me + step, n_col), me).start()
        return carry

    lax.fori_loop(1, n_col, send, 0)
    feat_copy = pltpu.make_async_remote_copy(
        src_ref=dst_ref, dst_ref=chip_ref.at[pl.ds(pl.multiple_of(core * half, half), half), :],
        send_sem=feat_send, recv_sem=feat_recv, device_id={"col": partner}, device_id_type=pl.DeviceIdType.MESH)
    feat_copy.start()

    slots = rows_ref.shape[1]
    row_block = rows_ref[...].astype(f32)
    slot = lax.broadcasted_iota(jnp.int32, (1, slots), 1)
    row_block = jnp.where(slot < count_ref[...], row_block, 255.0)
    pad = jnp.full((1, ORDER - slots), 255.0, f32)
    row_block = jnp.concatenate([row_block, pad], axis=1)
    across = jnp.broadcast_to(row_block, (ORDER, ORDER))
    down = jnp.transpose(across)
    lane = lax.broadcasted_iota(jnp.int32, (ORDER, ORDER), 1)
    sub = lax.broadcasted_iota(jnp.int32, (ORDER, ORDER), 0)
    before = jnp.sum(jnp.where((down == across) & (sub < lane), 1.0, 0.0), axis=0, keepdims=True)
    block_id = lax.broadcasted_iota(jnp.int32, (16, ORDER), 0).astype(f32)
    counts = jnp.sum(jnp.where(block_id == row_block, 1.0, 0.0), axis=1, keepdims=True)
    pairs = jnp.floor((counts + 1.0) * 0.5)
    start = jnp.sum(jnp.where(block_id < row_block, pairs, 0.0), axis=0, keepdims=True)
    place = jnp.where(row_block < 254.0, 2.0 * start + before, -1.0)
    place_down = jnp.transpose(jnp.broadcast_to(place, (ORDER, ORDER)))
    columns = jnp.concatenate([cols_ref[...].astype(f32), jnp.zeros((1, ORDER - slots), f32)], axis=1)
    lane_row = lax.broadcasted_iota(jnp.int32, (1, ORDER), 1).astype(f32)
    code = 1.0 + lane_row + 256.0 * columns + 8192.0 * jnp.minimum(row_block, 15.0)
    code_down = jnp.transpose(jnp.broadcast_to(code, (ORDER, ORDER)))
    found = jnp.sum(jnp.where(place_down == lane.astype(f32), code_down, 0.0), axis=0, keepdims=True)
    order_ref[...] = found.astype(jnp.int32)
    pairs_ref[...] = jnp.broadcast_to(jnp.sum(pairs, axis=0, keepdims=True), (1, 128)).astype(jnp.int32)

    def finish(step, carry):
        peer = lax.rem(me + step, n_col)
        done = score_copy(peer, peer)
        done.wait_send()
        done.wait_recv()
        return carry

    lax.fori_loop(1, n_col, finish, 0)
    feat_copy.wait()


def edges_kernel(order_ref, pairs_ref, score_ref, feat_ref, weight_ref, att_ref, mask_hbm,
                 out_ref, scaled, ratio, ratio_dst, src_score, dst_score, acc, masks, mask_sem):
    n_blocks = acc.shape[0]
    n_cols = scaled.shape[0]
    total = pairs_ref[0, 0]

    def decode(position):
        code = order_ref[0, position]
        index = jnp.maximum(code - 1, 0)
        return code, index & 255, (index >> 8) & 31, index >> 13

    def mask_copy(pair, side, slot_at):
        ring = lax.rem(pair, RING)
        return pltpu.make_async_copy(mask_hbm.at[slot_at], masks.at[ring, side], mask_sem.at[ring, side])

    def fetch(pair):
        first = decode(2 * pair)
        second = decode(2 * pair + 1)
        mask_copy(pair, 0, first[1]).start()

        @pl.when(second[0] > 0)
        def _():
            mask_copy(pair, 1, second[1]).start()

        @pl.when(second[0] == 0)
        def _():
            masks[lax.rem(pair, RING), 1] = jnp.zeros((TILE, TILE), jnp.int32)

    def arrive(pair):
        mask_copy(pair, 0, 0).wait()

        @pl.when(decode(2 * pair + 1)[0] > 0)
        def _():
            mask_copy(pair, 1, 0).wait()

    def prefetch(pair, carry):
        @pl.when(pair < total)
        def _():
            fetch(pair)
        return carry

    lax.fori_loop(0, RING - 1, prefetch, 0)

    column = attention_column(att_ref[...])

    def source_block(block, carry):
        low, high = carry
        at = pl.multiple_of(block * TILE, TILE)
        values = project_t(weight_ref[...], feat_ref[pl.ds(at, TILE), :]).astype(f32)
        rows = head_rows(values, column)
        pad = jnp.zeros((14, TILE), f32)
        for h in range(HEADS):
            grow = jnp.exp(rows[h])
            fall = jnp.exp(-0.8 * rows[h])
            grow_high = grow.astype(bf16).astype(f32)
            scaled[block, h, 0:HEAD_DIM, :] = (values[h * HEAD_DIM : (h + 1) * HEAD_DIM] * grow).astype(bf16)
            scaled[block, h, HEAD_DIM:AUG, :] = jnp.concatenate([grow_high, grow - grow_high, pad], axis=0).astype(bf16)
            ratio[block, h] = jnp.broadcast_to(fall, (16, TILE)).astype(bf16)
        stacked = jnp.concatenate(rows, axis=0)
        src_score[block] = stacked
        return jnp.minimum(low, stacked), jnp.maximum(high, stacked)

    low, high = lax.fori_loop(0, n_cols, source_block,
                              (jnp.full((HEADS, TILE), 1e30, f32), jnp.full((HEADS, TILE), -1e30, f32)))

    spread_head = lax.broadcasted_iota(jnp.int32, (HEADS, HEADS * TILE), 0)
    spread_lane = lax.broadcasted_iota(jnp.int32, (HEADS, HEADS * TILE), 1) // TILE
    spread = jnp.where(spread_head == spread_lane, 1.0, 0.0).astype(bf16)

    def dst_block(block, carry):
        low, high = carry
        score = score_ref[2 * block] + score_ref[2 * block + 1]
        dst_score[block] = score
        fall = jnp.exp(-0.8 * score).astype(bf16)
        wide = transposed_dot(fall, spread).astype(bf16)
        for h in range(HEADS):
            ratio_dst[block, h] = wide[:, h * TILE : (h + 1) * TILE]
        acc[block] = jnp.zeros(acc.shape[1:], f32)
        return jnp.minimum(low, score), jnp.maximum(high, score)

    low, high = lax.fori_loop(0, n_blocks, dst_block, (low, high))
    factored = (jnp.max(high) <= SPAN) & (jnp.min(low) >= -SPAN)

    @pl.when(factored)
    def _():
        def pair_step(pair, carry):
            @pl.when(pair + RING - 1 < total)
            def _():
                fetch(pair + RING - 1)

            arrive(pair)
            _, _, col_a, block = decode(2 * pair)
            _, _, col_b, _ = decode(2 * pair + 1)
            ring = lax.rem(pair, RING)
            mask_a = masks[ring, 0].astype(f32).astype(bf16).reshape(8, 16, TILE)
            mask_b = masks[ring, 1].astype(f32).astype(bf16).reshape(8, 16, TILE)
            one = jnp.ones((), bf16)
            for h in range(HEADS):
                fall_dst = ratio_dst[block, h].reshape(8, 16, TILE)
                weight_a = jnp.maximum(fall_dst * ratio[col_a, h][None], one) * mask_a
                weight_b = jnp.maximum(fall_dst * ratio[col_b, h][None], one) * mask_b
                edge = jnp.concatenate([weight_a.reshape(TILE, TILE), weight_b.reshape(TILE, TILE)], axis=1)
                source = jnp.concatenate([scaled[col_a, h], scaled[col_b, h]], axis=1)
                acc[block, h] += lax.dot_general(source, edge, (((1,), (1,)), ((), ())), preferred_element_type=f32)
            return carry

        lax.fori_loop(0, total, pair_step, 0)

        def reference_rows(block, carry):
            for h in range(HEADS):
                acc[block, h, 66:67, :] = dst_score[block, h : h + 1, :]
            return carry

        lax.fori_loop(0, n_blocks, reference_rows, 0)

    @pl.when(jnp.logical_not(factored))
    def _():
        def empty_rows(block, carry):
            for h in range(HEADS):
                acc[block, h, 66:67, :] = jnp.full((1, TILE), NEG, f32)
            return carry

        lax.fori_loop(0, n_blocks, empty_rows, 0)

        def one_tile(ring, side, col, block):
            present = jnp.transpose(masks[ring, side].astype(f32)) > 0.0
            at = pl.multiple_of(col * TILE, TILE)
            masks_free = project_t(weight_ref[...], feat_ref[pl.ds(at, TILE), :])
            for h in range(HEADS):
                source = as_column(src_score[col, h : h + 1, :], TILE)
                logit = leaky_relu(source + dst_score[block, h : h + 1, :])
                logit = jnp.where(present, logit, NEG)
                old_max = acc[block, h, 66:67, :]
                new_max = jnp.maximum(old_max, jnp.max(logit, axis=0, keepdims=True))
                prob = jnp.where(present, jnp.exp(logit - new_max), 0.0)
                keep = jnp.exp(old_max - new_max)
                message = jnp.dot(masks_free[h * HEAD_DIM : (h + 1) * HEAD_DIM], prob.astype(bf16),
                                  preferred_element_type=f32)
                acc[block, h, 0:HEAD_DIM, :] = acc[block, h, 0:HEAD_DIM, :] * keep + message
                acc[block, h, 64:65, :] = acc[block, h, 64:65, :] * keep + jnp.sum(prob, axis=0, keepdims=True)
                acc[block, h, 66:67, :] = new_max

        def pair_step(pair, carry):
            @pl.when(pair + RING - 1 < total)
            def _():
                fetch(pair + RING - 1)

            arrive(pair)
            ring = lax.rem(pair, RING)
            for side in range(2):
                _, _, col, _ = decode(2 * pair + side)
                one_tile(ring, side, col, decode(2 * pair)[3])
            return carry

        lax.fori_loop(0, total, pair_step, 0)

    def store_block(block, carry):
        for half in range(2):
            logs = []
            for g in range(HALF_HEADS):
                h = half * HALF_HEADS + g
                denominator = acc[block, h, 64:65, :] + acc[block, h, 65:66, :]
                some = denominator > 0.0
                safe = jnp.where(some, denominator, 1.0)
                out_ref[half, block, g * HEAD_DIM : (g + 1) * HEAD_DIM, :] = (
                    acc[block, h, 0:HEAD_DIM, :] * (1.0 / safe)).astype(bf16)
                logs.append(jnp.where(some, acc[block, h, 66:67, :] + jnp.log(safe), NEG))
            out_ref[half, block, HALF:BLOCK, :] = pack_logs(jnp.concatenate(logs, axis=0))
        return carry

    lax.fori_loop(0, n_blocks, store_block, 0)


def pack_logs(logs):
    high, middle, low = [part.astype(f32) for part in split3(logs)]
    return jnp.concatenate([high, middle, low, jnp.zeros_like(high)], axis=0).astype(bf16)


def unpack_logs(rows):
    wide = rows.astype(f32)
    n = HALF_HEADS
    return wide[0:n] + wide[n : 2 * n] + wide[2 * n : 3 * n]


def merge_blocks(blocks):
    logs = [unpack_logs(block[HALF:BLOCK]) for block in blocks]
    top = functools.reduce(jnp.maximum, logs)
    grow = [jnp.exp(log - top) for log in logs]
    total = functools.reduce(jnp.add, grow)
    share = [g * (1.0 / total) for g in grow]
    parts = []
    for h in range(HALF_HEADS):
        at = slice(h * HEAD_DIM, (h + 1) * HEAD_DIM)
        terms = [block[at].astype(f32) * s[h : h + 1] for block, s in zip(blocks, share)]
        parts.append(functools.reduce(jnp.add, terms).astype(bf16))
    return parts, pack_logs(top + jnp.log(total))


def store_block_parts(ref, index, merged):
    parts, logs = merged
    for h, part in enumerate(parts):
        ref[index + (slice(h * HEAD_DIM, (h + 1) * HEAD_DIM), slice(None))] = part
    ref[index + (slice(HALF, BLOCK), slice(None))] = logs


def merge_kernel(n_y, n_z, part_ref, chip_ref, weight_ref, att_src_ref, att_dst_ref, bias_ref, out_ref,
                 own, pair_in, summed, y_in, z_sum, z_in, self_values, self_logit, fin, fin_in,
                 own_sem, pair_send, pair_recv, y_send, y_recv, z_send, z_recv, fin_send, fin_recv):
    me = lax.axis_index("col")
    core = lax.rem(me, 2)
    chip = me // 2
    y = lax.rem(chip, n_y)
    z = chip // n_y
    partner = me + 1 - 2 * core

    def at(z_at, y_at):
        return {"col": (z_at * n_y + y_at) * 2 + core}

    mesh_id = pl.DeviceIdType.MESH
    barrier = pltpu.get_barrier_semaphore()
    pl.semaphore_signal(barrier, inc=1, device_id={"col": partner}, device_id_type=mesh_id)
    for step in range(1, n_y):
        pl.semaphore_signal(barrier, inc=1, device_id=at(z, lax.rem(y + step, n_y)), device_id_type=mesh_id)
    for step in range(1, n_z):
        pl.semaphore_signal(barrier, inc=1, device_id=at(lax.rem(z + step, n_z), y), device_id_type=mesh_id)

    def z_of(step):
        return lax.rem(z + 1 + step, n_z)

    def own_copy(step):
        rows = pl.ds(z_of(step) * n_y, n_y)
        return pltpu.make_async_copy(part_ref.at[core, rows], own.at[rows], own_sem.at[step])

    def pair_copy(step):
        rows = pl.ds(z_of(step) * n_y, n_y)
        return pltpu.make_async_remote_copy(
            src_ref=part_ref.at[1 - core, rows], dst_ref=pair_in.at[rows], send_sem=pair_send.at[step],
            recv_sem=pair_recv.at[step], device_id={"col": partner}, device_id_type=mesh_id)

    def y_copy(step, dy):
        block = z_of(step) * n_y + lax.rem(y + dy, n_y)
        return pltpu.make_async_remote_copy(
            src_ref=summed.at[block], dst_ref=y_in.at[step, dy - 1], send_sem=y_send.at[step, dy - 1],
            recv_sem=y_recv.at[step, dy - 1], device_id=at(z, lax.rem(y + dy, n_y)), device_id_type=mesh_id)

    def z_copy(step):
        return pltpu.make_async_remote_copy(
            src_ref=z_sum.at[step], dst_ref=z_in.at[step], send_sem=z_send.at[step],
            recv_sem=z_recv.at[step], device_id=at(z_of(step), y), device_id_type=mesh_id)

    for step in range(n_z):
        own_copy(step).start()

    values = project_t(weight_ref[...], chip_ref[...]).astype(f32)
    self_values[...] = values
    cross = jnp.concatenate(head_rows(values, attention_column(att_src_ref[...])), axis=0)
    direct = jnp.concatenate(head_rows(values, attention_column(att_dst_ref[...])), axis=0)
    logit = leaky_relu(cross + direct)
    self_logit[0] = logit
    self_logit[1] = jnp.concatenate([logit[HALF_HEADS:], logit[:HALF_HEADS]], axis=0)

    pl.semaphore_wait(barrier, 1 + (n_y - 1) + (n_z - 1))
    for step in range(n_z):
        pair_copy(step).start()

    def pair_merge(step):
        own_copy(step).wait()
        pair_copy(step).wait()
        for dy in range(n_y):
            block = z_of(step) * n_y + lax.rem(y + dy, n_y)
            store_block_parts(summed, (block,), merge_blocks([own[block], pair_in[block]]))
        for dy in range(1, n_y):
            y_copy(step, dy).start()

    def y_merge(step):
        for dy in range(1, n_y):
            y_copy(step, dy).wait()
        blocks = [summed[z_of(step) * n_y + y]] + [y_in[step, dy - 1] for dy in range(1, n_y)]
        store_block_parts(z_sum, (step,), merge_blocks(blocks))
        if step < n_z - 1:
            z_copy(step).start()

    for step in range(n_z):
        pair_merge(step)
        if step > 0:
            y_merge(step - 1)
    y_merge(n_z - 1)
    for step in range(n_z - 1):
        z_copy(step).wait()

    blocks = [z_sum[n_z - 1]] + [z_in[step] for step in range(n_z - 1)]
    logs = [unpack_logs(block[HALF:BLOCK]) for block in blocks] + [self_logit[core][0:HALF_HEADS]]
    top = functools.reduce(jnp.maximum, logs)
    grow = [jnp.exp(log - top) for log in logs]
    inverse = 1.0 / functools.reduce(jnp.add, grow)
    pieces = []
    for h in range(HALF_HEADS):
        rows = slice(h * HEAD_DIM, (h + 1) * HEAD_DIM)
        start = pl.multiple_of(core * HALF, HALF) + h * HEAD_DIM
        terms = [block[rows].astype(f32) * g[h : h + 1] for block, g in zip(blocks, grow)]
        terms.append(self_values[pl.ds(start, HEAD_DIM), :] * grow[-1][h : h + 1])
        pieces.append(functools.reduce(jnp.add, terms) * inverse[h : h + 1])
    mixed = jnp.transpose(jnp.concatenate(pieces, axis=0))
    bias = jnp.where(core == 0, bias_ref[:, 0:HALF], bias_ref[:, HALF:FEAT])
    mixed = mixed + bias
    fin[...] = jnp.where(mixed > 0, mixed, jnp.exp(jnp.minimum(mixed, 0.0)) - 1.0)
    half = out_ref.shape[0]
    final = pltpu.make_async_remote_copy(
        src_ref=fin.at[pl.ds(pl.multiple_of((1 - core) * half, half), half), :], dst_ref=fin_in,
        send_sem=fin_send, recv_sem=fin_recv, device_id={"col": partner}, device_id_type=mesh_id)
    final.start()
    mine = fin[pl.ds(pl.multiple_of(core * half, half), half), :]
    final.wait()
    theirs = fin_in[...]
    out_ref[:, 0:HALF] = jnp.where(core == 0, mine, theirs)
    out_ref[:, HALF:FEAT] = jnp.where(core == 0, theirs, mine)


VMEM = pl.BlockSpec(memory_space=pltpu.VMEM)
SMEM = pl.BlockSpec(memory_space=pltpu.SMEM)
ANY = pl.BlockSpec(memory_space=pl.ANY)
DMA = pltpu.SemaphoreType.DMA


def destination_scores(n_col, dst_feat, weight, att_dst, tile_rows, tile_cols, tile_count):
    own = dst_feat.shape[0]
    return pl.pallas_call(
        functools.partial(scores_kernel, n_col),
        name="destination_scores",
        out_shape=(
            jax.ShapeDtypeStruct((n_col, HEADS, 2 * own), f32),
            jax.ShapeDtypeStruct((2 * own, dst_feat.shape[1]), bf16),
            jax.ShapeDtypeStruct((1, ORDER), jnp.int32),
            jax.ShapeDtypeStruct((1, 128), jnp.int32),
        ),
        in_specs=[VMEM] * 6,
        out_specs=(VMEM,) * 4,
        scratch_shapes=[pltpu.VMEM((HEADS, 2 * own), f32), DMA((n_col,)), DMA((n_col,)), DMA(()), DMA(())],
        compiler_params=pltpu.CompilerParams(collective_id=0, has_side_effects=True,
                                             vmem_limit_bytes=16 * 1024 * 1024),
    )(dst_feat, weight, att_dst, tile_rows, tile_cols, tile_count)


def edge_sums(order, pairs, scores, src_feat, weight, att_src, masks):
    n_cols = src_feat.shape[0] // TILE
    n_blocks = scores.shape[0] // 2
    return pl.pallas_call(
        edges_kernel,
        name="edge_sums",
        out_shape=jax.ShapeDtypeStruct((2, n_blocks, BLOCK, TILE), bf16),
        in_specs=[SMEM, SMEM, VMEM, VMEM, VMEM, VMEM, ANY],
        out_specs=VMEM,
        scratch_shapes=[
            pltpu.VMEM((n_cols, HEADS, AUG, TILE), bf16),
            pltpu.VMEM((n_cols, HEADS, 16, TILE), bf16),
            pltpu.VMEM((n_blocks, HEADS, TILE, TILE), bf16),
            pltpu.VMEM((n_cols, HEADS, TILE), f32),
            pltpu.VMEM((n_blocks, HEADS, TILE), f32),
            pltpu.VMEM((n_blocks, HEADS, AUG, TILE), f32),
            pltpu.VMEM((RING, 2, TILE, TILE), jnp.int32),
            DMA((RING, 2)),
        ],
        compiler_params=pltpu.CompilerParams(vmem_limit_bytes=48 * 1024 * 1024),
    )(order, pairs, scores, src_feat, weight, att_src, masks)


def merge(n_y, n_z, parts, chip_feat, weight, att_src, att_dst, bias):
    n_blocks = n_y * n_z
    own = chip_feat.shape[0] // 2
    return pl.pallas_call(
        functools.partial(merge_kernel, n_y, n_z),
        name="merge",
        out_shape=jax.ShapeDtypeStruct((own, FEAT), f32),
        in_specs=[ANY, VMEM, VMEM, VMEM, VMEM, VMEM],
        out_specs=VMEM,
        scratch_shapes=[
            pltpu.VMEM((n_blocks, BLOCK, TILE), bf16),
            pltpu.VMEM((n_blocks, BLOCK, TILE), bf16),
            pltpu.VMEM((n_blocks, BLOCK, TILE), bf16),
            pltpu.VMEM((n_z, n_y - 1, BLOCK, TILE), bf16),
            pltpu.VMEM((n_z, BLOCK, TILE), bf16),
            pltpu.VMEM((n_z - 1, BLOCK, TILE), bf16),
            pltpu.VMEM((FEAT, TILE), f32),
            pltpu.VMEM((2, HEADS, TILE), f32),
            pltpu.VMEM((TILE, HALF), f32),
            pltpu.VMEM((own, HALF), f32),
            DMA((n_z,)), DMA((n_z,)), DMA((n_z,)), DMA((n_z, n_y - 1)), DMA((n_z, n_y - 1)),
            DMA((n_z - 1,)), DMA((n_z - 1,)), DMA(()), DMA(()),
        ],
        compiler_params=pltpu.CompilerParams(collective_id=1, has_side_effects=True,
                                             vmem_limit_bytes=32 * 1024 * 1024),
    )(parts, chip_feat, weight, att_src, att_dst, bias)


def local(n_col, src_feat, dst_feat, weight, att_src, att_dst, bias, tile_rows, tile_cols, tile_masks, tile_count):
    slots = tile_rows.shape[2]
    scores, chip_feat, order, pairs = destination_scores(
        n_col, dst_feat, weight, att_dst, tile_rows.reshape(1, slots), tile_cols.reshape(1, slots), tile_count)
    parts = edge_sums(order, pairs, scores, src_feat, weight, att_src, tile_masks.reshape(slots, TILE, TILE))
    n_y = 4
    return merge(n_y, n_col // (2 * n_y), parts, chip_feat, weight, att_src, att_dst, bias.reshape(1, FEAT))


def solution(mesh):
    placed = (
        P("col", None),
        P(("row", "col"), None),
        P(),
        P(),
        P(),
        P(),
        P("row", "col", None),
        P("row", "col", None),
        P("row", "col", None, None, None),
        P("row", "col"),
    )
    return jax.shard_map(
        functools.partial(local, mesh.shape["col"]), mesh=mesh, in_specs=placed,
        out_specs=P(("row", "col"), None), check_vma=False,
    )
```

```python
import functools

import jax
import jax.numpy as jnp
from jax import lax
from jax.experimental import pallas as pl
from jax.experimental.pallas import tpu as pltpu
from jax.sharding import PartitionSpec as P

HEADS = 8
HEAD_DIM = 64
TILE = 128
FEAT = HEADS * HEAD_DIM
NEG = -1e30
SPAN = 50.0
HALF = FEAT // 2
HALF_HEADS = HEADS // 2
BLOCK = HALF + 16
AUG = HEAD_DIM + 16
GROUP = 4
RING = 16
ORDER = 256

f32 = jnp.float32
bf16 = jnp.bfloat16


def leaky_relu(values):
    return jnp.maximum(values, 0.2 * values)


def split3(values):
    high = values.astype(bf16)
    rest = values - high.astype(f32)
    middle = rest.astype(bf16)
    low = (rest - middle.astype(f32)).astype(bf16)
    return high, middle, low


def transposed_dot(left, right):
    return lax.dot_general(left, right, (((0,), (0,)), ((), ())), preferred_element_type=f32)


def project_t(weight, features):
    return lax.dot_general(weight, features, (((0,), (1,)), ((), ())), preferred_element_type=f32).astype(bf16)


def project_rows_t(weight_t, features):
    return lax.dot_general(weight_t, features, (((1,), (1,)), ((), ())), preferred_element_type=f32).astype(bf16)


def attention_column(attention):
    wide = jnp.concatenate([attention] * HEADS, axis=1)
    head = lax.broadcasted_iota(jnp.int32, wide.shape, 0)
    lane_head = lax.broadcasted_iota(jnp.int32, wide.shape, 1) // HEAD_DIM
    wide = jnp.where(head == lane_head, wide, 0.0)
    terms = jnp.concatenate([part.astype(f32) for part in split3(wide)], axis=0).astype(bf16)
    return transposed_dot(terms, jnp.ones((terms.shape[0], 128), bf16))


def head_rows(values, column):
    product = values * column
    return [
        jnp.sum(product[h * HEAD_DIM : (h + 1) * HEAD_DIM], axis=0, keepdims=True) for h in range(HEADS)
    ]


def as_column(row, rows):
    return jnp.transpose(jnp.broadcast_to(row, (rows, row.shape[1])))


def scores_kernel(n_col, dst_hbm, weight_hbm, att_src_hbm, att_dst_hbm, rows_hbm, cols_hbm, count_hbm, feat_hbm,
                  score_ref, self_ref, cross_ref, order_ref, pairs_ref, scaled, ratio, src_score, range_ref,
                  dst_in, weight_in, att_src_in, att_dst_in, rows_in, cols_in, count_in, feat_in,
                  own, own_cross, own_self, weight_t, spread,
                  load_sem, send_sem, recv_sem, part_send, part_recv):
    me = lax.axis_index("col")
    core = lax.rem(me, 2)
    partner = me + 1 - 2 * core
    loads = [
        pltpu.make_async_copy(source, target, load_sem.at[i])
        for i, (source, target) in enumerate([
            (weight_hbm, weight_in), (dst_hbm, dst_in), (att_src_hbm, att_src_in), (att_dst_hbm, att_dst_in),
            (rows_hbm, rows_in), (cols_hbm, cols_in), (count_hbm, count_in), (feat_hbm, feat_in)])
    ]
    for load in loads:
        load.start()
    barrier = pltpu.get_barrier_semaphore()

    def greet(step, carry):
        pl.semaphore_signal(barrier, inc=1, device_id={"col": lax.rem(me + step, n_col)},
                            device_id_type=pl.DeviceIdType.MESH)
        return carry

    lax.fori_loop(1, n_col, greet, 0)
    for load in loads[:-1]:
        load.wait()

    weight_t[...] = jnp.transpose(weight_in[...])
    column = attention_column(att_src_in[...])
    features = dst_in[...]
    both = jnp.concatenate([features, features], axis=0)
    side = lax.broadcasted_iota(jnp.int32, both.shape, 0) // features.shape[0]
    both = jnp.where(side == core, both, jnp.zeros_like(both))
    values = project_rows_t(weight_t[...], both)
    wide = values.astype(f32)
    own[...] = jnp.concatenate(head_rows(wide, attention_column(att_dst_in[...])), axis=0)
    own_cross[...] = jnp.concatenate(head_rows(wide, column), axis=0)
    own_self[...] = values
    spread[...] = column
    score_ref[me] = own[...]
    cross_ref[0] = own_cross[...]
    self_ref[0] = own_self[pl.ds(pl.multiple_of(core * HALF, HALF), HALF), :]

    pl.semaphore_wait(barrier, n_col - 1)

    def score_copy(target, source_slot):
        return pltpu.make_async_remote_copy(
            src_ref=own, dst_ref=score_ref.at[me], send_sem=send_sem.at[target], recv_sem=recv_sem.at[source_slot],
            device_id={"col": target}, device_id_type=pl.DeviceIdType.MESH)

    def send(step, carry):
        score_copy(lax.rem(me + step, n_col), me).start()
        return carry

    lax.fori_loop(1, n_col, send, 0)
    self_copy = pltpu.make_async_remote_copy(
        src_ref=own_self.at[pl.ds(pl.multiple_of((1 - core) * HALF, HALF), HALF), :], dst_ref=self_ref.at[1],
        send_sem=part_send.at[0], recv_sem=part_recv.at[0],
        device_id={"col": partner}, device_id_type=pl.DeviceIdType.MESH)
    cross_copy = pltpu.make_async_remote_copy(
        src_ref=own_cross, dst_ref=cross_ref.at[1], send_sem=part_send.at[1], recv_sem=part_recv.at[1],
        device_id={"col": partner}, device_id_type=pl.DeviceIdType.MESH)
    self_copy.start()
    cross_copy.start()

    loads[-1].wait()
    n_cols = scaled.shape[0]
    wide_block = 2 * TILE

    def source_block(step, carry):
        low, high = carry
        at = pl.multiple_of(step * wide_block, wide_block)
        values = project_rows_t(weight_t[...], feat_in[pl.ds(at, wide_block), :]).astype(f32)
        pad = jnp.zeros((14, TILE), f32)
        for part in range(2):
            block = 2 * step + part
            here = values[:, part * TILE : (part + 1) * TILE]
            rows = head_rows(here, spread[...])
            for h in range(HEADS):
                grow = jnp.exp(rows[h])
                fall = jnp.exp(-0.8 * rows[h])
                grow_high = grow.astype(bf16).astype(f32)
                scaled[block, h, 0:HEAD_DIM, :] = (here[h * HEAD_DIM : (h + 1) * HEAD_DIM] * grow).astype(bf16)
                scaled[block, h, HEAD_DIM:AUG, :] = jnp.concatenate(
                    [grow_high, grow - grow_high, pad], axis=0).astype(bf16)
                ratio[block, h] = jnp.broadcast_to(fall, (16, TILE)).astype(bf16)
            stacked = jnp.concatenate(rows, axis=0)
            src_score[block] = stacked
            low, high = jnp.minimum(low, stacked), jnp.maximum(high, stacked)
        return low, high

    low, high = lax.fori_loop(0, n_cols // 2, source_block,
                              (jnp.full((HEADS, TILE), 1e30, f32), jnp.full((HEADS, TILE), -1e30, f32)))
    range_ref[0] = low
    range_ref[1] = high

    slots = rows_in.shape[1]
    row_block = rows_in[...].astype(f32)
    slot = lax.broadcasted_iota(jnp.int32, (1, slots), 1)
    row_block = jnp.where(slot < count_in[...], row_block, 255.0)
    pad = jnp.full((1, ORDER - slots), 255.0, f32)
    row_block = jnp.concatenate([row_block, pad], axis=1)
    across = jnp.broadcast_to(row_block, (ORDER, ORDER))
    down = jnp.transpose(across)
    lane = lax.broadcasted_iota(jnp.int32, (ORDER, ORDER), 1)
    sub = lax.broadcasted_iota(jnp.int32, (ORDER, ORDER), 0)
    before = jnp.sum(jnp.where((down == across) & (sub < lane), 1.0, 0.0), axis=0, keepdims=True)
    block_id = lax.broadcasted_iota(jnp.int32, (16, ORDER), 0).astype(f32)
    counts = jnp.sum(jnp.where(block_id == row_block, 1.0, 0.0), axis=1, keepdims=True)
    pairs = jnp.floor((counts + 1.0) * 0.5)
    start = jnp.sum(jnp.where(block_id < row_block, pairs, 0.0), axis=0, keepdims=True)
    place = jnp.where(row_block < 254.0, 2.0 * start + before, -1.0)
    place_down = jnp.transpose(jnp.broadcast_to(place, (ORDER, ORDER)))
    columns = jnp.concatenate([cols_in[...].astype(f32), jnp.zeros((1, ORDER - slots), f32)], axis=1)
    lane_row = lax.broadcasted_iota(jnp.int32, (1, ORDER), 1).astype(f32)
    code = 1.0 + lane_row + 256.0 * columns + 8192.0 * jnp.minimum(row_block, 15.0)
    code_down = jnp.transpose(jnp.broadcast_to(code, (ORDER, ORDER)))
    found = jnp.sum(jnp.where(place_down == lane.astype(f32), code_down, 0.0), axis=0, keepdims=True)
    order_ref[...] = found.astype(jnp.int32)
    pairs_ref[...] = jnp.broadcast_to(jnp.sum(pairs, axis=0, keepdims=True), (1, 128)).astype(jnp.int32)

    def finish(step, carry):
        peer = lax.rem(me + step, n_col)
        done = score_copy(peer, peer)
        done.wait_send()
        done.wait_recv()
        return carry

    lax.fori_loop(1, n_col, finish, 0)
    self_copy.wait()
    cross_copy.wait()


def edges_kernel(order_ref, pairs_ref, score_ref, scaled, ratio, src_score, range_ref, feat_hbm, weight_hbm, mask_hbm,
                 out_ref, ratio_dst, dst_score, acc, masks, feat_in, weight_in, mask_sem, load_sem):
    n_blocks = acc.shape[0]
    total = pairs_ref[0, 0]
    groups = (total + GROUP - 1) // GROUP

    def decode(position):
        code = order_ref[0, position]
        index = jnp.maximum(code - 1, 0)
        return code, index & 255, (index >> 8) & 31, index >> 13

    def mask_copy(pair, side, slot_at):
        ring = lax.rem(pair, RING)
        return pltpu.make_async_copy(mask_hbm.at[slot_at], masks.at[ring, side], mask_sem.at[ring, side])

    def fetch(pair):
        for side in range(2):
            code, slot, _, _ = decode(2 * pair + side)

            @pl.when(code > 0)
            def _(side=side, slot=slot):
                mask_copy(pair, side, slot).start()

            @pl.when(code == 0)
            def _(side=side):
                masks[lax.rem(pair, RING), side] = jnp.zeros((TILE, TILE), jnp.int32)

    def arrive(pair):
        for side in range(2):
            @pl.when(decode(2 * pair + side)[0] > 0)
            def _(side=side):
                mask_copy(pair, side, 0).wait()

    def prefetch(pair, carry):
        fetch(pair)
        return carry

    lax.fori_loop(0, jnp.minimum(groups * GROUP, RING - GROUP), prefetch, 0)

    spread_head = lax.broadcasted_iota(jnp.int32, (HEADS, HEADS * TILE), 0)
    spread_lane = lax.broadcasted_iota(jnp.int32, (HEADS, HEADS * TILE), 1) // TILE
    spread = jnp.where(spread_head == spread_lane, 1.0, 0.0).astype(bf16)

    def dst_block(step, carry):
        low, high = carry
        for part in range(4):
            block = 4 * step + part
            score = score_ref[2 * block] + score_ref[2 * block + 1]
            dst_score[block] = score
            fall = jnp.exp(-0.8 * score).astype(bf16)
            wide = transposed_dot(fall, spread).astype(bf16)
            for h in range(HEADS):
                ratio_dst[block, h] = wide[:, h * TILE : (h + 1) * TILE]
            acc[block] = jnp.zeros(acc.shape[1:], f32)
            low, high = jnp.minimum(low, score), jnp.maximum(high, score)
        return low, high

    low, high = lax.fori_loop(0, n_blocks // 4, dst_block, (range_ref[0], range_ref[1]))
    factored = (jnp.max(high) <= SPAN) & (jnp.min(low) >= -SPAN)

    def next_group(group):
        for step in range(GROUP):
            pair = group * GROUP + step

            @pl.when(pair + RING - GROUP < groups * GROUP)
            def _():
                fetch(pair + RING - GROUP)

            arrive(pair)

    @pl.when(factored)
    def _():
        def group_step(group, carry):
            next_group(group)
            one = jnp.ones((), bf16)
            for step in range(GROUP):
                pair = group * GROUP + step
                _, _, col_a, block = decode(2 * pair)
                _, _, col_b, _ = decode(2 * pair + 1)
                ring = lax.rem(pair, RING)
                mask_a = masks[ring, 0].astype(f32).astype(bf16).reshape(8, 16, TILE)
                mask_b = masks[ring, 1].astype(f32).astype(bf16).reshape(8, 16, TILE)
                for h in range(HEADS):
                    fall_dst = ratio_dst[block, h].reshape(8, 16, TILE)
                    weight_a = jnp.maximum(fall_dst * ratio[col_a, h][None], one) * mask_a
                    weight_b = jnp.maximum(fall_dst * ratio[col_b, h][None], one) * mask_b
                    edge = jnp.concatenate([weight_a.reshape(TILE, TILE), weight_b.reshape(TILE, TILE)], axis=1)
                    source = jnp.concatenate([scaled[col_a, h], scaled[col_b, h]], axis=1)
                    acc[block, h] += lax.dot_general(source, edge, (((1,), (1,)), ((), ())),
                                                     preferred_element_type=f32)
            return carry

        lax.fori_loop(0, groups, group_step, 0)

        def reference_rows(block, carry):
            for h in range(HEADS):
                acc[block, h, 66:67, :] = dst_score[block, h : h + 1, :]
            return carry

        lax.fori_loop(0, n_blocks, reference_rows, 0)

    @pl.when(jnp.logical_not(factored))
    def _():
        loads = [pltpu.make_async_copy(feat_hbm, feat_in, load_sem.at[0]),
                 pltpu.make_async_copy(weight_hbm, weight_in, load_sem.at[1])]
        for load in loads:
            load.start()
        for load in loads:
            load.wait()

        def empty_rows(block, carry):
            for h in range(HEADS):
                acc[block, h, 66:67, :] = jnp.full((1, TILE), NEG, f32)
            return carry

        lax.fori_loop(0, n_blocks, empty_rows, 0)

        def one_tile(ring, side, col, block):
            present = jnp.transpose(masks[ring, side].astype(f32)) > 0.0
            at = pl.multiple_of(col * TILE, TILE)
            values = project_t(weight_in[...], feat_in[pl.ds(at, TILE), :])
            for h in range(HEADS):
                source = as_column(src_score[col, h : h + 1, :], TILE)
                logit = leaky_relu(source + dst_score[block, h : h + 1, :])
                logit = jnp.where(present, logit, NEG)
                old_max = acc[block, h, 66:67, :]
                new_max = jnp.maximum(old_max, jnp.max(logit, axis=0, keepdims=True))
                prob = jnp.where(present, jnp.exp(logit - new_max), 0.0)
                keep = jnp.exp(old_max - new_max)
                message = jnp.dot(values[h * HEAD_DIM : (h + 1) * HEAD_DIM], prob.astype(bf16),
                                  preferred_element_type=f32)
                acc[block, h, 0:HEAD_DIM, :] = acc[block, h, 0:HEAD_DIM, :] * keep + message
                acc[block, h, 64:65, :] = acc[block, h, 64:65, :] * keep + jnp.sum(prob, axis=0, keepdims=True)
                acc[block, h, 66:67, :] = new_max

        def group_step(group, carry):
            next_group(group)

            def pair_step(step, inner):
                pair = group * GROUP + step
                ring = lax.rem(pair, RING)
                for side in range(2):
                    _, _, col, _ = decode(2 * pair + side)
                    one_tile(ring, side, col, decode(2 * pair)[3])
                return inner

            return lax.fori_loop(0, GROUP, pair_step, carry)

        lax.fori_loop(0, groups, group_step, 0)

    def store_block(step, carry):
        for part in range(2):
            block = 2 * step + part
            for half in range(2):
                logs = []
                for g in range(HALF_HEADS):
                    h = half * HALF_HEADS + g
                    denominator = acc[block, h, 64:65, :] + acc[block, h, 65:66, :]
                    some = denominator > 0.0
                    safe = jnp.where(some, denominator, 1.0)
                    out_ref[half, block, g * HEAD_DIM : (g + 1) * HEAD_DIM, :] = (
                        acc[block, h, 0:HEAD_DIM, :] * (1.0 / safe)).astype(bf16)
                    logs.append(jnp.where(some, acc[block, h, 66:67, :] + jnp.log(safe), NEG))
                out_ref[half, block, HALF:BLOCK, :] = pack_logs(jnp.concatenate(logs, axis=0))
        return carry

    lax.fori_loop(0, n_blocks // 2, store_block, 0)


def pack_logs(logs):
    high, middle, low = [part.astype(f32) for part in split3(logs)]
    return jnp.concatenate([high, middle, low, jnp.zeros_like(high)], axis=0).astype(bf16)


def unpack_logs(rows):
    wide = rows.astype(f32)
    n = HALF_HEADS
    return wide[0:n] + wide[n : 2 * n] + wide[2 * n : 3 * n]


def merge_blocks(blocks):
    logs = [unpack_logs(block[HALF:BLOCK]) for block in blocks]
    top = functools.reduce(jnp.maximum, logs)
    grow = [jnp.exp(log - top) for log in logs]
    total = functools.reduce(jnp.add, grow)
    share = [g * (1.0 / total) for g in grow]
    parts = []
    for h in range(HALF_HEADS):
        at = slice(h * HEAD_DIM, (h + 1) * HEAD_DIM)
        terms = [block[at].astype(f32) * s[h : h + 1] for block, s in zip(blocks, share)]
        parts.append(functools.reduce(jnp.add, terms).astype(bf16))
    return parts, pack_logs(top + jnp.log(total))


def store_block_parts(ref, index, merged):
    parts, logs = merged
    for h, part in enumerate(parts):
        ref[index + (slice(h * HEAD_DIM, (h + 1) * HEAD_DIM), slice(None))] = part
    ref[index + (slice(HALF, BLOCK), slice(None))] = logs


def merge_kernel(n_y, n_z, part_ref, score_ref, self_ref, cross_ref, bias_hbm, out_ref,
                 pair_in, summed, y_in, z_sum, z_in, self_logit, bias_in, fin, fin_in,
                 load_sem, pair_send, pair_recv, y_send, y_recv, z_send, z_recv, fin_send, fin_recv):
    me = lax.axis_index("col")
    core = lax.rem(me, 2)
    chip = me // 2
    y = lax.rem(chip, n_y)
    z = chip // n_y
    partner = me + 1 - 2 * core

    def at(z_at, y_at):
        return {"col": (z_at * n_y + y_at) * 2 + core}

    mesh_id = pl.DeviceIdType.MESH
    barrier = pltpu.get_barrier_semaphore()
    pl.semaphore_signal(barrier, inc=1, device_id={"col": partner}, device_id_type=mesh_id)
    for step in range(1, n_y):
        pl.semaphore_signal(barrier, inc=1, device_id=at(z, lax.rem(y + step, n_y)), device_id_type=mesh_id)
    for step in range(1, n_z):
        pl.semaphore_signal(barrier, inc=1, device_id=at(lax.rem(z + step, n_z), y), device_id_type=mesh_id)

    def z_of(step):
        return lax.rem(z + 1 + step, n_z)

    def pair_copy(step):
        rows = pl.ds(z_of(step) * n_y, n_y)
        return pltpu.make_async_remote_copy(
            src_ref=part_ref.at[1 - core, rows], dst_ref=pair_in.at[rows], send_sem=pair_send.at[step],
            recv_sem=pair_recv.at[step], device_id={"col": partner}, device_id_type=mesh_id)

    def y_copy(step, dy):
        block = z_of(step) * n_y + lax.rem(y + dy, n_y)
        return pltpu.make_async_remote_copy(
            src_ref=summed.at[block], dst_ref=y_in.at[step, dy - 1], send_sem=y_send.at[step, dy - 1],
            recv_sem=y_recv.at[step, dy - 1], device_id=at(z, lax.rem(y + dy, n_y)), device_id_type=mesh_id)

    def z_copy(step):
        return pltpu.make_async_remote_copy(
            src_ref=z_sum.at[step], dst_ref=z_in.at[step], send_sem=z_send.at[step],
            recv_sem=z_recv.at[step], device_id=at(z_of(step), y), device_id_type=mesh_id)

    bias_copy = pltpu.make_async_copy(bias_hbm, bias_in, load_sem)
    bias_copy.start()
    direct = score_ref[2 * chip] + score_ref[2 * chip + 1]
    logit = leaky_relu(direct + (cross_ref[0] + cross_ref[1]))
    self_logit[0] = logit
    self_logit[1] = jnp.concatenate([logit[HALF_HEADS:], logit[:HALF_HEADS]], axis=0)

    pl.semaphore_wait(barrier, 1 + (n_y - 1) + (n_z - 1))
    for step in range(n_z):
        pair_copy(step).start()

    def pair_merge(step):
        pair_copy(step).wait()
        for dy in range(n_y):
            block = z_of(step) * n_y + lax.rem(y + dy, n_y)
            store_block_parts(summed, (block,), merge_blocks([part_ref[core, block], pair_in[block]]))
        for dy in range(1, n_y):
            y_copy(step, dy).start()

    def y_merge(step):
        for dy in range(1, n_y):
            y_copy(step, dy).wait()
        blocks = [summed[z_of(step) * n_y + y]] + [y_in[step, dy - 1] for dy in range(1, n_y)]
        store_block_parts(z_sum, (step,), merge_blocks(blocks))
        if step < n_z - 1:
            z_copy(step).start()

    for step in range(n_z):
        pair_merge(step)
        if step > 0:
            y_merge(step - 1)
    y_merge(n_z - 1)
    for step in range(n_z - 1):
        z_copy(step).wait()

    blocks = [z_sum[n_z - 1]] + [z_in[step] for step in range(n_z - 1)]
    logs = [unpack_logs(block[HALF:BLOCK]) for block in blocks] + [self_logit[core][0:HALF_HEADS]]
    top = functools.reduce(jnp.maximum, logs)
    grow = [jnp.exp(log - top) for log in logs]
    inverse = 1.0 / functools.reduce(jnp.add, grow)
    pieces = []
    for h in range(HALF_HEADS):
        rows = slice(h * HEAD_DIM, (h + 1) * HEAD_DIM)
        terms = [block[rows].astype(f32) * g[h : h + 1] for block, g in zip(blocks, grow)]
        mine = self_ref[0, rows, :].astype(f32) + self_ref[1, rows, :].astype(f32)
        terms.append(mine * grow[-1][h : h + 1])
        pieces.append(functools.reduce(jnp.add, terms) * inverse[h : h + 1])
    mixed = jnp.transpose(jnp.concatenate(pieces, axis=0))
    bias_copy.wait()
    bias = jnp.where(core == 0, bias_in[:, 0:HALF], bias_in[:, HALF:FEAT])
    mixed = mixed + bias
    fin[...] = jnp.where(mixed > 0, mixed, jnp.exp(jnp.minimum(mixed, 0.0)) - 1.0)
    half = out_ref.shape[0]
    final = pltpu.make_async_remote_copy(
        src_ref=fin.at[pl.ds(pl.multiple_of((1 - core) * half, half), half), :], dst_ref=fin_in,
        send_sem=fin_send, recv_sem=fin_recv, device_id={"col": partner}, device_id_type=mesh_id)
    final.start()
    mine = fin[pl.ds(pl.multiple_of(core * half, half), half), :]
    final.wait()
    theirs = fin_in[...]
    out_ref[:, 0:HALF] = jnp.where(core == 0, mine, theirs)
    out_ref[:, HALF:FEAT] = jnp.where(core == 0, theirs, mine)


VMEM = pl.BlockSpec(memory_space=pltpu.VMEM)
SMEM = pl.BlockSpec(memory_space=pltpu.SMEM)
HBM = pl.BlockSpec(memory_space=pltpu.HBM)
DMA = pltpu.SemaphoreType.DMA


MIB = 1024 * 1024


def scores_and_tables(n_col, dst_feat, weight, att_src, att_dst, tile_rows, tile_cols, tile_count, src_feat):
    own = dst_feat.shape[0]
    chip = 2 * own
    n_cols = src_feat.shape[0] // TILE
    return pl.pallas_call(
        functools.partial(scores_kernel, n_col),
        name="scores_and_tables",
        out_shape=(
            jax.ShapeDtypeStruct((n_col, HEADS, chip), f32),
            jax.ShapeDtypeStruct((2, HALF, chip), bf16),
            jax.ShapeDtypeStruct((2, HEADS, chip), f32),
            jax.ShapeDtypeStruct((1, ORDER), jnp.int32),
            jax.ShapeDtypeStruct((1, 128), jnp.int32),
            jax.ShapeDtypeStruct((n_cols, HEADS, AUG, TILE), bf16),
            jax.ShapeDtypeStruct((n_cols, HEADS, 16, TILE), bf16),
            jax.ShapeDtypeStruct((n_cols, HEADS, TILE), f32),
            jax.ShapeDtypeStruct((2, HEADS, TILE), f32),
        ),
        in_specs=[HBM] * 8,
        out_specs=(VMEM,) * 9,
        scratch_shapes=[
            pltpu.VMEM(dst_feat.shape, bf16), pltpu.VMEM(weight.shape, bf16),
            pltpu.VMEM(att_src.shape, f32), pltpu.VMEM(att_dst.shape, f32),
            pltpu.VMEM(tile_rows.shape, jnp.int32), pltpu.VMEM(tile_cols.shape, jnp.int32),
            pltpu.VMEM(tile_count.shape, jnp.int32), pltpu.VMEM(src_feat.shape, bf16),
            pltpu.VMEM((HEADS, chip), f32), pltpu.VMEM((HEADS, chip), f32), pltpu.VMEM((FEAT, chip), bf16),
            pltpu.VMEM((FEAT, weight.shape[0]), bf16), pltpu.VMEM((FEAT, TILE), f32),
            DMA((8,)), DMA((n_col,)), DMA((n_col,)), DMA((2,)), DMA((2,)),
        ],
        compiler_params=pltpu.CompilerParams(collective_id=0, has_side_effects=True, vmem_limit_bytes=40 * MIB),
    )(dst_feat, weight, att_src, att_dst, tile_rows, tile_cols, tile_count, src_feat)


def edge_sums(order, pairs, scores, scaled, ratio, src_score, span, src_feat, weight, masks):
    n_blocks = scores.shape[0] // 2
    return pl.pallas_call(
        edges_kernel,
        name="edge_sums",
        out_shape=jax.ShapeDtypeStruct((2, n_blocks, BLOCK, TILE), bf16),
        in_specs=[SMEM, SMEM] + [VMEM] * 5 + [HBM] * 3,
        out_specs=VMEM,
        scratch_shapes=[
            pltpu.VMEM((n_blocks, HEADS, TILE, TILE), bf16),
            pltpu.VMEM((n_blocks, HEADS, TILE), f32),
            pltpu.VMEM((n_blocks, HEADS, AUG, TILE), f32),
            pltpu.VMEM((RING, 2, TILE, TILE), jnp.int32),
            pltpu.VMEM(src_feat.shape, bf16),
            pltpu.VMEM(weight.shape, bf16),
            DMA((RING, 2)), DMA((2,)),
        ],
        compiler_params=pltpu.CompilerParams(vmem_limit_bytes=40 * MIB),
    )(order, pairs, scores, scaled, ratio, src_score, span, src_feat, weight, masks)


def merge(n_y, n_z, parts, scores, self_values, cross, bias):
    n_blocks = n_y * n_z
    own = scores.shape[2] // 2
    return pl.pallas_call(
        functools.partial(merge_kernel, n_y, n_z),
        name="merge",
        out_shape=jax.ShapeDtypeStruct((own, FEAT), f32),
        in_specs=[VMEM] * 4 + [HBM],
        out_specs=VMEM,
        scratch_shapes=[
            pltpu.VMEM((n_blocks, BLOCK, TILE), bf16),
            pltpu.VMEM((n_blocks, BLOCK, TILE), bf16),
            pltpu.VMEM((n_z, n_y - 1, BLOCK, TILE), bf16),
            pltpu.VMEM((n_z, BLOCK, TILE), bf16),
            pltpu.VMEM((n_z - 1, BLOCK, TILE), bf16),
            pltpu.VMEM((2, HEADS, TILE), f32),
            pltpu.VMEM((1, FEAT), f32),
            pltpu.VMEM((TILE, HALF), f32),
            pltpu.VMEM((own, HALF), f32),
            DMA(()), DMA((n_z,)), DMA((n_z,)), DMA((n_z, n_y - 1)), DMA((n_z, n_y - 1)),
            DMA((n_z - 1,)), DMA((n_z - 1,)), DMA(()), DMA(()),
        ],
        compiler_params=pltpu.CompilerParams(collective_id=1, has_side_effects=True, vmem_limit_bytes=40 * MIB),
    )(parts, scores, self_values, cross, bias)


def local(n_col, src_feat, dst_feat, weight, att_src, att_dst, bias, tile_rows, tile_cols, tile_masks, tile_count):
    slots = tile_rows.shape[2]
    tile_rows, tile_cols, bias = tile_rows.reshape(1, slots), tile_cols.reshape(1, slots), bias.reshape(1, FEAT)
    tile_masks = tile_masks.reshape(slots, TILE, TILE)
    (src_feat, dst_feat, weight, att_src, att_dst, bias, tile_rows, tile_cols, tile_masks) = [
        pltpu.with_memory_space_constraint(array, pltpu.HBM)
        for array in (src_feat, dst_feat, weight, att_src, att_dst, bias, tile_rows, tile_cols, tile_masks)
    ]
    scores, self_values, cross, order, pairs, scaled, ratio, src_score, span = scores_and_tables(
        n_col, dst_feat, weight, att_src, att_dst, tile_rows, tile_cols, tile_count, src_feat)
    parts = edge_sums(order, pairs, scores, scaled, ratio, src_score, span, src_feat, weight, tile_masks)
    n_y = 4
    return merge(n_y, n_col // (2 * n_y), parts, scores, self_values, cross, bias)


def solution(mesh):
    placed = (
        P("col", None),
        P(("row", "col"), None),
        P(),
        P(),
        P(),
        P(),
        P("row", "col", None),
        P("row", "col", None),
        P("row", "col", None, None, None),
        P("row", "col"),
    )
    return jax.shard_map(
        functools.partial(local, mesh.shape["col"]), mesh=mesh, in_specs=placed,
        out_specs=P(("row", "col"), None), check_vma=False,
    )
```

```python
import functools

import jax
import jax.numpy as jnp
from jax import lax
from jax.experimental import pallas as pl
from jax.experimental.pallas import tpu as pltpu
from jax.sharding import PartitionSpec as P

HEADS = 8
HEAD_DIM = 64
TILE = 128
FEAT = HEADS * HEAD_DIM
NEG = -1e30
SPAN = 50.0
HALF = FEAT // 2
HALF_HEADS = HEADS // 2
BLOCK = HALF + 16
AUG = HEAD_DIM + 16
GROUP = 8
RING = 32
ORDER = 256

f32 = jnp.float32
bf16 = jnp.bfloat16


def leaky_relu(values):
    return jnp.maximum(values, 0.2 * values)


def split3(values):
    high = values.astype(bf16)
    rest = values - high.astype(f32)
    middle = rest.astype(bf16)
    low = (rest - middle.astype(f32)).astype(bf16)
    return high, middle, low


def transposed_dot(left, right):
    return lax.dot_general(left, right, (((0,), (0,)), ((), ())), preferred_element_type=f32)


def project_t(weight, features):
    return lax.dot_general(weight, features, (((0,), (1,)), ((), ())), preferred_element_type=f32).astype(bf16)


def project_rows_t(weight_t, features):
    return lax.dot_general(weight_t, features, (((1,), (1,)), ((), ())), preferred_element_type=f32).astype(bf16)


def attention_column(attention):
    wide = jnp.concatenate([attention] * HEADS, axis=1)
    head = lax.broadcasted_iota(jnp.int32, wide.shape, 0)
    lane_head = lax.broadcasted_iota(jnp.int32, wide.shape, 1) // HEAD_DIM
    wide = jnp.where(head == lane_head, wide, 0.0)
    terms = jnp.concatenate([part.astype(f32) for part in split3(wide)], axis=0).astype(bf16)
    return transposed_dot(terms, jnp.ones((terms.shape[0], 128), bf16))


def head_rows(values, column):
    product = values * column
    return [
        jnp.sum(product[h * HEAD_DIM : (h + 1) * HEAD_DIM], axis=0, keepdims=True) for h in range(HEADS)
    ]


def as_column(row, rows):
    return jnp.transpose(jnp.broadcast_to(row, (rows, row.shape[1])))


def scores_kernel(n_col, dst_hbm, weight_hbm, att_src_hbm, att_dst_hbm, rows_hbm, cols_hbm, count_hbm, feat_hbm,
                  score_ref, self_ref, cross_ref, order_ref, pairs_ref, scaled, ratio, src_score, range_ref,
                  dst_in, weight_in, att_src_in, att_dst_in, rows_in, cols_in, count_in, feat_in,
                  own, own_cross, own_self, weight_t, spread,
                  load_sem, send_sem, recv_sem, part_send, part_recv):
    me = lax.axis_index("col")
    core = lax.rem(me, 2)
    partner = me + 1 - 2 * core
    loads = [
        pltpu.make_async_copy(source, target, load_sem.at[i])
        for i, (source, target) in enumerate([
            (weight_hbm, weight_in), (dst_hbm, dst_in), (att_src_hbm, att_src_in), (att_dst_hbm, att_dst_in),
            (rows_hbm, rows_in), (cols_hbm, cols_in), (count_hbm, count_in), (feat_hbm, feat_in)])
    ]
    for load in loads:
        load.start()
    barrier = pltpu.get_barrier_semaphore()

    def greet(step, carry):
        pl.semaphore_signal(barrier, inc=1, device_id={"col": lax.rem(me + step, n_col)},
                            device_id_type=pl.DeviceIdType.MESH)
        return carry

    lax.fori_loop(1, n_col, greet, 0)
    for load in loads[:-1]:
        load.wait()

    weight_t[...] = jnp.transpose(weight_in[...])
    column = attention_column(att_src_in[...])
    features = dst_in[...]
    both = jnp.concatenate([features, features], axis=0)
    side = lax.broadcasted_iota(jnp.int32, both.shape, 0) // features.shape[0]
    both = jnp.where(side == core, both, jnp.zeros_like(both))
    values = project_rows_t(weight_t[...], both)
    wide = values.astype(f32)
    own[...] = jnp.concatenate(head_rows(wide, attention_column(att_dst_in[...])), axis=0)
    own_cross[...] = jnp.concatenate(head_rows(wide, column), axis=0)
    own_self[...] = values
    spread[...] = column
    score_ref[me] = own[...]
    cross_ref[0] = own_cross[...]
    self_ref[0] = own_self[pl.ds(pl.multiple_of(core * HALF, HALF), HALF), :]

    pl.semaphore_wait(barrier, n_col - 1)

    def score_copy(target, source_slot):
        return pltpu.make_async_remote_copy(
            src_ref=own, dst_ref=score_ref.at[me], send_sem=send_sem.at[target], recv_sem=recv_sem.at[source_slot],
            device_id={"col": target}, device_id_type=pl.DeviceIdType.MESH)

    def send(step, carry):
        score_copy(lax.rem(me + step, n_col), me).start()
        return carry

    lax.fori_loop(1, n_col, send, 0)
    self_copy = pltpu.make_async_remote_copy(
        src_ref=own_self.at[pl.ds(pl.multiple_of((1 - core) * HALF, HALF), HALF), :], dst_ref=self_ref.at[1],
        send_sem=part_send.at[0], recv_sem=part_recv.at[0],
        device_id={"col": partner}, device_id_type=pl.DeviceIdType.MESH)
    cross_copy = pltpu.make_async_remote_copy(
        src_ref=own_cross, dst_ref=cross_ref.at[1], send_sem=part_send.at[1], recv_sem=part_recv.at[1],
        device_id={"col": partner}, device_id_type=pl.DeviceIdType.MESH)
    self_copy.start()
    cross_copy.start()

    loads[-1].wait()
    n_cols = scaled.shape[0]
    wide_block = 2 * TILE

    def source_block(step, carry):
        low, high = carry
        at = pl.multiple_of(step * wide_block, wide_block)
        values = project_rows_t(weight_t[...], feat_in[pl.ds(at, wide_block), :]).astype(f32)
        pad = jnp.zeros((14, TILE), f32)
        for part in range(2):
            block = 2 * step + part
            here = values[:, part * TILE : (part + 1) * TILE]
            rows = head_rows(here, spread[...])
            for h in range(HEADS):
                grow = jnp.exp(rows[h])
                fall = jnp.exp(-0.8 * rows[h])
                grow_high = grow.astype(bf16).astype(f32)
                scaled[block, h, 0:HEAD_DIM, :] = (here[h * HEAD_DIM : (h + 1) * HEAD_DIM] * grow).astype(bf16)
                scaled[block, h, HEAD_DIM:AUG, :] = jnp.concatenate(
                    [grow_high, grow - grow_high, pad], axis=0).astype(bf16)
                ratio[block, h] = jnp.broadcast_to(fall, (16, TILE)).astype(bf16)
            stacked = jnp.concatenate(rows, axis=0)
            src_score[block] = stacked
            low, high = jnp.minimum(low, stacked), jnp.maximum(high, stacked)
        return low, high

    low, high = lax.fori_loop(0, n_cols // 2, source_block,
                              (jnp.full((HEADS, TILE), 1e30, f32), jnp.full((HEADS, TILE), -1e30, f32)))
    range_ref[0] = low
    range_ref[1] = high

    slots = rows_in.shape[1]
    row_block = rows_in[...].astype(f32)
    slot = lax.broadcasted_iota(jnp.int32, (1, slots), 1)
    row_block = jnp.where(slot < count_in[...], row_block, 255.0)
    pad = jnp.full((1, ORDER - slots), 255.0, f32)
    row_block = jnp.concatenate([row_block, pad], axis=1)
    across = jnp.broadcast_to(row_block, (ORDER, ORDER))
    down = jnp.transpose(across)
    lane = lax.broadcasted_iota(jnp.int32, (ORDER, ORDER), 1)
    sub = lax.broadcasted_iota(jnp.int32, (ORDER, ORDER), 0)
    before = jnp.sum(jnp.where((down == across) & (sub < lane), 1.0, 0.0), axis=0, keepdims=True)
    block_id = lax.broadcasted_iota(jnp.int32, (16, ORDER), 0).astype(f32)
    counts = jnp.sum(jnp.where(block_id == row_block, 1.0, 0.0), axis=1, keepdims=True)
    pairs = jnp.floor((counts + 1.0) * 0.5)
    start = jnp.sum(jnp.where(block_id < row_block, pairs, 0.0), axis=0, keepdims=True)
    place = jnp.where(row_block < 254.0, 2.0 * start + before, -1.0)
    place_down = jnp.transpose(jnp.broadcast_to(place, (ORDER, ORDER)))
    columns = jnp.concatenate([cols_in[...].astype(f32), jnp.zeros((1, ORDER - slots), f32)], axis=1)
    lane_row = lax.broadcasted_iota(jnp.int32, (1, ORDER), 1).astype(f32)
    code = 1.0 + lane_row + 256.0 * columns + 8192.0 * jnp.minimum(row_block, 15.0)
    code_down = jnp.transpose(jnp.broadcast_to(code, (ORDER, ORDER)))
    found = jnp.sum(jnp.where(place_down == lane.astype(f32), code_down, 0.0), axis=0, keepdims=True)
    order_ref[...] = found.astype(jnp.int32)
    pairs_ref[...] = jnp.broadcast_to(jnp.sum(pairs, axis=0, keepdims=True), (1, 128)).astype(jnp.int32)

    def finish(step, carry):
        peer = lax.rem(me + step, n_col)
        done = score_copy(peer, peer)
        done.wait_send()
        done.wait_recv()
        return carry

    lax.fori_loop(1, n_col, finish, 0)
    self_copy.wait()
    cross_copy.wait()


def edges_kernel(order_ref, pairs_ref, score_ref, scaled, ratio, src_score, range_ref, feat_hbm, weight_hbm, mask_hbm,
                 out_ref, ratio_dst, dst_score, acc, masks, feat_in, weight_in, mask_sem, load_sem):
    n_blocks = acc.shape[0]
    total = pairs_ref[0, 0]
    groups = (total + GROUP - 1) // GROUP

    def decode(position):
        code = order_ref[0, position]
        index = jnp.maximum(code - 1, 0)
        return code, index & 255, (index >> 8) & 31, index >> 13

    def fetch(pair):
        ring = lax.rem(pair, RING)
        for side in range(2):
            slot = decode(2 * pair + side)[1]
            pltpu.make_async_copy(mask_hbm.at[slot], masks.at[ring, side], mask_sem.at[ring]).start()

    def arrive(pair):
        ring = lax.rem(pair, RING)
        pltpu.make_async_copy(mask_hbm.at[pl.ds(0, 2)], masks.at[ring], mask_sem.at[ring]).wait()

    def mask_of(ring, side, code):
        return masks[ring, side].astype(f32) * jnp.minimum(code, 1).astype(f32)

    def prefetch(pair, carry):
        fetch(pair)
        return carry

    lax.fori_loop(0, jnp.minimum(groups * GROUP, RING - GROUP), prefetch, 0)

    spread_head = lax.broadcasted_iota(jnp.int32, (HEADS, HEADS * TILE), 0)
    spread_lane = lax.broadcasted_iota(jnp.int32, (HEADS, HEADS * TILE), 1) // TILE
    spread = jnp.where(spread_head == spread_lane, 1.0, 0.0).astype(bf16)

    def dst_block(step, carry):
        low, high = carry
        for part in range(4):
            block = 4 * step + part
            score = score_ref[2 * block] + score_ref[2 * block + 1]
            dst_score[block] = score
            fall = jnp.exp(-0.8 * score).astype(bf16)
            wide = transposed_dot(fall, spread).astype(bf16)
            for h in range(HEADS):
                ratio_dst[block, h] = wide[:, h * TILE : (h + 1) * TILE]
            acc[block] = jnp.zeros(acc.shape[1:], f32)
            low, high = jnp.minimum(low, score), jnp.maximum(high, score)
        return low, high

    low, high = lax.fori_loop(0, n_blocks // 4, dst_block, (range_ref[0], range_ref[1]))
    factored = (jnp.max(high) <= SPAN) & (jnp.min(low) >= -SPAN)

    def next_group(group):
        @pl.when((group + 1) * GROUP + RING - 2 * GROUP < groups * GROUP)
        def _():
            for step in range(GROUP):
                fetch(group * GROUP + step + RING - GROUP)

        for step in range(GROUP):
            arrive(group * GROUP + step)

    @pl.when(factored)
    def _():
        def group_step(group, carry):
            next_group(group)
            one = jnp.ones((), bf16)
            for step in range(GROUP):
                pair = group * GROUP + step
                code_a, _, col_a, block = decode(2 * pair)
                code_b, _, col_b, _ = decode(2 * pair + 1)
                ring = lax.rem(pair, RING)
                mask_a = mask_of(ring, 0, code_a).astype(bf16).reshape(8, 16, TILE)
                mask_b = mask_of(ring, 1, code_b).astype(bf16).reshape(8, 16, TILE)
                for h in range(HEADS):
                    fall_dst = ratio_dst[block, h].reshape(8, 16, TILE)
                    weight_a = jnp.maximum(fall_dst * ratio[col_a, h][None], one) * mask_a
                    weight_b = jnp.maximum(fall_dst * ratio[col_b, h][None], one) * mask_b
                    edge = jnp.concatenate([weight_a.reshape(TILE, TILE), weight_b.reshape(TILE, TILE)], axis=1)
                    source = jnp.concatenate([scaled[col_a, h], scaled[col_b, h]], axis=1)
                    acc[block, h] += lax.dot_general(source, edge, (((1,), (1,)), ((), ())),
                                                     preferred_element_type=f32)
            return carry

        lax.fori_loop(0, groups, group_step, 0)

        def reference_rows(block, carry):
            for h in range(HEADS):
                acc[block, h, 66:67, :] = dst_score[block, h : h + 1, :]
            return carry

        lax.fori_loop(0, n_blocks, reference_rows, 0)

    @pl.when(jnp.logical_not(factored))
    def _():
        loads = [pltpu.make_async_copy(feat_hbm, feat_in, load_sem.at[0]),
                 pltpu.make_async_copy(weight_hbm, weight_in, load_sem.at[1])]
        for load in loads:
            load.start()
        for load in loads:
            load.wait()

        def empty_rows(block, carry):
            for h in range(HEADS):
                acc[block, h, 66:67, :] = jnp.full((1, TILE), NEG, f32)
            return carry

        lax.fori_loop(0, n_blocks, empty_rows, 0)

        def one_tile(ring, side, code, col, block):
            present = jnp.transpose(mask_of(ring, side, code)) > 0.0
            at = pl.multiple_of(col * TILE, TILE)
            values = project_t(weight_in[...], feat_in[pl.ds(at, TILE), :])
            for h in range(HEADS):
                source = as_column(src_score[col, h : h + 1, :], TILE)
                logit = leaky_relu(source + dst_score[block, h : h + 1, :])
                logit = jnp.where(present, logit, NEG)
                old_max = acc[block, h, 66:67, :]
                new_max = jnp.maximum(old_max, jnp.max(logit, axis=0, keepdims=True))
                prob = jnp.where(present, jnp.exp(logit - new_max), 0.0)
                keep = jnp.exp(old_max - new_max)
                message = jnp.dot(values[h * HEAD_DIM : (h + 1) * HEAD_DIM], prob.astype(bf16),
                                  preferred_element_type=f32)
                acc[block, h, 0:HEAD_DIM, :] = acc[block, h, 0:HEAD_DIM, :] * keep + message
                acc[block, h, 64:65, :] = acc[block, h, 64:65, :] * keep + jnp.sum(prob, axis=0, keepdims=True)
                acc[block, h, 66:67, :] = new_max

        def group_step(group, carry):
            next_group(group)

            def pair_step(step, inner):
                pair = group * GROUP + step
                ring = lax.rem(pair, RING)
                for side in range(2):
                    code, _, col, _ = decode(2 * pair + side)
                    one_tile(ring, side, code, col, decode(2 * pair)[3])
                return inner

            return lax.fori_loop(0, GROUP, pair_step, carry)

        lax.fori_loop(0, groups, group_step, 0)

    def store_block(step, carry):
        for part in range(2):
            block = 2 * step + part
            for half in range(2):
                logs = []
                for g in range(HALF_HEADS):
                    h = half * HALF_HEADS + g
                    denominator = acc[block, h, 64:65, :] + acc[block, h, 65:66, :]
                    some = denominator > 0.0
                    safe = jnp.where(some, denominator, 1.0)
                    out_ref[half, block, g * HEAD_DIM : (g + 1) * HEAD_DIM, :] = (
                        acc[block, h, 0:HEAD_DIM, :] * (1.0 / safe)).astype(bf16)
                    logs.append(jnp.where(some, acc[block, h, 66:67, :] + jnp.log(safe), NEG))
                out_ref[half, block, HALF:BLOCK, :] = pack_logs(jnp.concatenate(logs, axis=0))
        return carry

    lax.fori_loop(0, n_blocks // 2, store_block, 0)


def pack_logs(logs):
    high, middle, low = [part.astype(f32) for part in split3(logs)]
    return jnp.concatenate([high, middle, low, jnp.zeros_like(high)], axis=0).astype(bf16)


def unpack_logs(rows):
    wide = rows.astype(f32)
    n = HALF_HEADS
    return wide[0:n] + wide[n : 2 * n] + wide[2 * n : 3 * n]


def merge_blocks(blocks):
    logs = [unpack_logs(block[HALF:BLOCK]) for block in blocks]
    top = functools.reduce(jnp.maximum, logs)
    grow = [jnp.exp(log - top) for log in logs]
    total = functools.reduce(jnp.add, grow)
    share = [g * (1.0 / total) for g in grow]
    parts = []
    for h in range(HALF_HEADS):
        at = slice(h * HEAD_DIM, (h + 1) * HEAD_DIM)
        terms = [block[at].astype(f32) * s[h : h + 1] for block, s in zip(blocks, share)]
        parts.append(functools.reduce(jnp.add, terms).astype(bf16))
    return parts, pack_logs(top + jnp.log(total))


def store_block_parts(ref, index, merged):
    parts, logs = merged
    for h, part in enumerate(parts):
        ref[index + (slice(h * HEAD_DIM, (h + 1) * HEAD_DIM), slice(None))] = part
    ref[index + (slice(HALF, BLOCK), slice(None))] = logs


def merge_kernel(n_y, n_z, part_ref, score_ref, self_ref, cross_ref, bias_hbm, out_ref,
                 pair_in, summed, y_in, z_sum, z_in, self_logit, bias_in, fin, fin_in,
                 load_sem, pair_send, pair_recv, y_send, y_recv, z_send, z_recv, fin_send, fin_recv):
    me = lax.axis_index("col")
    core = lax.rem(me, 2)
    chip = me // 2
    y = lax.rem(chip, n_y)
    z = chip // n_y
    partner = me + 1 - 2 * core

    def at(z_at, y_at):
        return {"col": (z_at * n_y + y_at) * 2 + core}

    mesh_id = pl.DeviceIdType.MESH
    barrier = pltpu.get_barrier_semaphore()
    pl.semaphore_signal(barrier, inc=1, device_id={"col": partner}, device_id_type=mesh_id)
    for step in range(1, n_y):
        pl.semaphore_signal(barrier, inc=1, device_id=at(z, lax.rem(y + step, n_y)), device_id_type=mesh_id)
    for step in range(1, n_z):
        pl.semaphore_signal(barrier, inc=1, device_id=at(lax.rem(z + step, n_z), y), device_id_type=mesh_id)

    def z_of(step):
        return lax.rem(z + 1 + step, n_z)

    def pair_copy(step):
        rows = pl.ds(z_of(step) * n_y, n_y)
        return pltpu.make_async_remote_copy(
            src_ref=part_ref.at[1 - core, rows], dst_ref=pair_in.at[rows], send_sem=pair_send.at[step],
            recv_sem=pair_recv.at[step], device_id={"col": partner}, device_id_type=mesh_id)

    def y_copy(step, dy):
        block = z_of(step) * n_y + lax.rem(y + dy, n_y)
        return pltpu.make_async_remote_copy(
            src_ref=summed.at[block], dst_ref=y_in.at[step, dy - 1], send_sem=y_send.at[step, dy - 1],
            recv_sem=y_recv.at[step, dy - 1], device_id=at(z, lax.rem(y + dy, n_y)), device_id_type=mesh_id)

    def z_copy(step):
        return pltpu.make_async_remote_copy(
            src_ref=z_sum.at[step], dst_ref=z_in.at[step], send_sem=z_send.at[step],
            recv_sem=z_recv.at[step], device_id=at(z_of(step), y), device_id_type=mesh_id)

    bias_copy = pltpu.make_async_copy(bias_hbm, bias_in, load_sem)
    bias_copy.start()
    direct = score_ref[2 * chip] + score_ref[2 * chip + 1]
    logit = leaky_relu(direct + (cross_ref[0] + cross_ref[1]))
    self_logit[0] = logit
    self_logit[1] = jnp.concatenate([logit[HALF_HEADS:], logit[:HALF_HEADS]], axis=0)

    pl.semaphore_wait(barrier, 1 + (n_y - 1) + (n_z - 1))
    for step in range(n_z):
        pair_copy(step).start()

    def pair_merge(step):
        pair_copy(step).wait()
        for dy in range(n_y):
            block = z_of(step) * n_y + lax.rem(y + dy, n_y)
            store_block_parts(summed, (block,), merge_blocks([part_ref[core, block], pair_in[block]]))
        for dy in range(1, n_y):
            y_copy(step, dy).start()

    def y_merge(step):
        for dy in range(1, n_y):
            y_copy(step, dy).wait()
        blocks = [summed[z_of(step) * n_y + y]] + [y_in[step, dy - 1] for dy in range(1, n_y)]
        store_block_parts(z_sum, (step,), merge_blocks(blocks))
        if step < n_z - 1:
            z_copy(step).start()

    for step in range(n_z):
        pair_merge(step)
        if step > 0:
            y_merge(step - 1)
    y_merge(n_z - 1)
    for step in range(n_z - 1):
        z_copy(step).wait()

    blocks = [z_sum[n_z - 1]] + [z_in[step] for step in range(n_z - 1)]
    logs = [unpack_logs(block[HALF:BLOCK]) for block in blocks] + [self_logit[core][0:HALF_HEADS]]
    top = functools.reduce(jnp.maximum, logs)
    grow = [jnp.exp(log - top) for log in logs]
    inverse = 1.0 / functools.reduce(jnp.add, grow)
    pieces = []
    for h in range(HALF_HEADS):
        rows = slice(h * HEAD_DIM, (h + 1) * HEAD_DIM)
        terms = [block[rows].astype(f32) * g[h : h + 1] for block, g in zip(blocks, grow)]
        mine = self_ref[0, rows, :].astype(f32) + self_ref[1, rows, :].astype(f32)
        terms.append(mine * grow[-1][h : h + 1])
        pieces.append(functools.reduce(jnp.add, terms) * inverse[h : h + 1])
    mixed = jnp.transpose(jnp.concatenate(pieces, axis=0))
    bias_copy.wait()
    bias = jnp.where(core == 0, bias_in[:, 0:HALF], bias_in[:, HALF:FEAT])
    mixed = mixed + bias
    fin[...] = jnp.where(mixed > 0, mixed, jnp.exp(jnp.minimum(mixed, 0.0)) - 1.0)
    half = out_ref.shape[0]
    final = pltpu.make_async_remote_copy(
        src_ref=fin.at[pl.ds(pl.multiple_of((1 - core) * half, half), half), :], dst_ref=fin_in,
        send_sem=fin_send, recv_sem=fin_recv, device_id={"col": partner}, device_id_type=mesh_id)
    final.start()
    mine = fin[pl.ds(pl.multiple_of(core * half, half), half), :]
    final.wait()
    theirs = fin_in[...]
    out_ref[:, 0:HALF] = jnp.where(core == 0, mine, theirs)
    out_ref[:, HALF:FEAT] = jnp.where(core == 0, theirs, mine)


VMEM = pl.BlockSpec(memory_space=pltpu.VMEM)
SMEM = pl.BlockSpec(memory_space=pltpu.SMEM)
HBM = pl.BlockSpec(memory_space=pltpu.HBM)
DMA = pltpu.SemaphoreType.DMA


MIB = 1024 * 1024


def scores_and_tables(n_col, dst_feat, weight, att_src, att_dst, tile_rows, tile_cols, tile_count, src_feat):
    own = dst_feat.shape[0]
    chip = 2 * own
    n_cols = src_feat.shape[0] // TILE
    return pl.pallas_call(
        functools.partial(scores_kernel, n_col),
        name="scores_and_tables",
        out_shape=(
            jax.ShapeDtypeStruct((n_col, HEADS, chip), f32),
            jax.ShapeDtypeStruct((2, HALF, chip), bf16),
            jax.ShapeDtypeStruct((2, HEADS, chip), f32),
            jax.ShapeDtypeStruct((1, ORDER), jnp.int32),
            jax.ShapeDtypeStruct((1, 128), jnp.int32),
            jax.ShapeDtypeStruct((n_cols, HEADS, AUG, TILE), bf16),
            jax.ShapeDtypeStruct((n_cols, HEADS, 16, TILE), bf16),
            jax.ShapeDtypeStruct((n_cols, HEADS, TILE), f32),
            jax.ShapeDtypeStruct((2, HEADS, TILE), f32),
        ),
        in_specs=[HBM] * 8,
        out_specs=(VMEM,) * 9,
        scratch_shapes=[
            pltpu.VMEM(dst_feat.shape, bf16), pltpu.VMEM(weight.shape, bf16),
            pltpu.VMEM(att_src.shape, f32), pltpu.VMEM(att_dst.shape, f32),
            pltpu.VMEM(tile_rows.shape, jnp.int32), pltpu.VMEM(tile_cols.shape, jnp.int32),
            pltpu.VMEM(tile_count.shape, jnp.int32), pltpu.VMEM(src_feat.shape, bf16),
            pltpu.VMEM((HEADS, chip), f32), pltpu.VMEM((HEADS, chip), f32), pltpu.VMEM((FEAT, chip), bf16),
            pltpu.VMEM((FEAT, weight.shape[0]), bf16), pltpu.VMEM((FEAT, TILE), f32),
            DMA((8,)), DMA((n_col,)), DMA((n_col,)), DMA((2,)), DMA((2,)),
        ],
        compiler_params=pltpu.CompilerParams(collective_id=0, has_side_effects=True, vmem_limit_bytes=40 * MIB),
    )(dst_feat, weight, att_src, att_dst, tile_rows, tile_cols, tile_count, src_feat)


def edge_sums(order, pairs, scores, scaled, ratio, src_score, span, src_feat, weight, masks):
    n_blocks = scores.shape[0] // 2
    return pl.pallas_call(
        edges_kernel,
        name="edge_sums",
        out_shape=jax.ShapeDtypeStruct((2, n_blocks, BLOCK, TILE), bf16),
        in_specs=[SMEM, SMEM] + [VMEM] * 5 + [HBM] * 3,
        out_specs=VMEM,
        scratch_shapes=[
            pltpu.VMEM((n_blocks, HEADS, TILE, TILE), bf16),
            pltpu.VMEM((n_blocks, HEADS, TILE), f32),
            pltpu.VMEM((n_blocks, HEADS, AUG, TILE), f32),
            pltpu.VMEM((RING, 2, TILE, TILE), jnp.int32),
            pltpu.VMEM(src_feat.shape, bf16),
            pltpu.VMEM(weight.shape, bf16),
            DMA((RING,)), DMA((2,)),
        ],
        compiler_params=pltpu.CompilerParams(vmem_limit_bytes=40 * MIB),
    )(order, pairs, scores, scaled, ratio, src_score, span, src_feat, weight, masks)


def merge(n_y, n_z, parts, scores, self_values, cross, bias):
    n_blocks = n_y * n_z
    own = scores.shape[2] // 2
    return pl.pallas_call(
        functools.partial(merge_kernel, n_y, n_z),
        name="merge",
        out_shape=jax.ShapeDtypeStruct((own, FEAT), f32),
        in_specs=[VMEM] * 4 + [HBM],
        out_specs=VMEM,
        scratch_shapes=[
            pltpu.VMEM((n_blocks, BLOCK, TILE), bf16),
            pltpu.VMEM((n_blocks, BLOCK, TILE), bf16),
            pltpu.VMEM((n_z, n_y - 1, BLOCK, TILE), bf16),
            pltpu.VMEM((n_z, BLOCK, TILE), bf16),
            pltpu.VMEM((n_z - 1, BLOCK, TILE), bf16),
            pltpu.VMEM((2, HEADS, TILE), f32),
            pltpu.VMEM((1, FEAT), f32),
            pltpu.VMEM((TILE, HALF), f32),
            pltpu.VMEM((own, HALF), f32),
            DMA(()), DMA((n_z,)), DMA((n_z,)), DMA((n_z, n_y - 1)), DMA((n_z, n_y - 1)),
            DMA((n_z - 1,)), DMA((n_z - 1,)), DMA(()), DMA(()),
        ],
        compiler_params=pltpu.CompilerParams(collective_id=1, has_side_effects=True, vmem_limit_bytes=40 * MIB),
    )(parts, scores, self_values, cross, bias)


def local(n_col, src_feat, dst_feat, weight, att_src, att_dst, bias, tile_rows, tile_cols, tile_masks, tile_count):
    slots = tile_rows.shape[2]
    tile_rows, tile_cols, bias = tile_rows.reshape(1, slots), tile_cols.reshape(1, slots), bias.reshape(1, FEAT)
    tile_masks = tile_masks.reshape(slots, TILE, TILE)
    (src_feat, dst_feat, weight, att_src, att_dst, bias, tile_rows, tile_cols, tile_masks) = [
        pltpu.with_memory_space_constraint(array, pltpu.HBM)
        for array in (src_feat, dst_feat, weight, att_src, att_dst, bias, tile_rows, tile_cols, tile_masks)
    ]
    scores, self_values, cross, order, pairs, scaled, ratio, src_score, span = scores_and_tables(
        n_col, dst_feat, weight, att_src, att_dst, tile_rows, tile_cols, tile_count, src_feat)
    parts = edge_sums(order, pairs, scores, scaled, ratio, src_score, span, src_feat, weight, tile_masks)
    n_y = 4
    return merge(n_y, n_col // (2 * n_y), parts, scores, self_values, cross, bias)


def solution(mesh):
    placed = (
        P("col", None),
        P(("row", "col"), None),
        P(),
        P(),
        P(),
        P(),
        P("row", "col", None),
        P("row", "col", None),
        P("row", "col", None, None, None),
        P("row", "col"),
    )
    return jax.shard_map(
        functools.partial(local, mesh.shape["col"]), mesh=mesh, in_specs=placed,
        out_specs=P(("row", "col"), None), check_vma=False,
    )
```

```python
import functools

import jax
import jax.numpy as jnp
from jax import lax
from jax.experimental import pallas as pl
from jax.experimental.pallas import tpu as pltpu
from jax.sharding import PartitionSpec as P

HEADS = 8
HEAD_DIM = 64
TILE = 128
FEAT = HEADS * HEAD_DIM
NEG = -1e30
SPAN = 50.0
HALF = FEAT // 2
HALF_HEADS = HEADS // 2
BLOCK = HALF + 16
AUG = HEAD_DIM + 16
GROUP = 8
RING = 32
ORDER = 256

f32 = jnp.float32
bf16 = jnp.bfloat16


def leaky_relu(values):
    return jnp.maximum(values, 0.2 * values)


def split3(values):
    high = values.astype(bf16)
    rest = values - high.astype(f32)
    middle = rest.astype(bf16)
    low = (rest - middle.astype(f32)).astype(bf16)
    return high, middle, low


def transposed_dot(left, right):
    return lax.dot_general(left, right, (((0,), (0,)), ((), ())), preferred_element_type=f32)


def project_t(weight, features):
    return lax.dot_general(weight, features, (((0,), (1,)), ((), ())), preferred_element_type=f32).astype(bf16)


def project_rows_t(weight_t, features):
    return lax.dot_general(weight_t, features, (((1,), (1,)), ((), ())), preferred_element_type=f32).astype(bf16)


def attention_column(attention):
    wide = jnp.concatenate([attention] * HEADS, axis=1)
    head = lax.broadcasted_iota(jnp.int32, wide.shape, 0)
    lane_head = lax.broadcasted_iota(jnp.int32, wide.shape, 1) // HEAD_DIM
    wide = jnp.where(head == lane_head, wide, 0.0)
    terms = jnp.concatenate([part.astype(f32) for part in split3(wide)], axis=0).astype(bf16)
    return transposed_dot(terms, jnp.ones((terms.shape[0], 128), bf16))


def head_rows(values, column):
    product = values * column
    return [
        jnp.sum(product[h * HEAD_DIM : (h + 1) * HEAD_DIM], axis=0, keepdims=True) for h in range(HEADS)
    ]


def as_column(row, rows):
    return jnp.transpose(jnp.broadcast_to(row, (rows, row.shape[1])))


def scores_kernel(n_y, n_z, dst_hbm, weight_hbm, att_src_hbm, att_dst_hbm, rows_hbm, cols_hbm, count_hbm, feat_hbm,
                  score_ref, self_ref, cross_ref, order_ref, pairs_ref, scaled, ratio, src_score, range_ref,
                  dst_in, weight_in, att_src_in, att_dst_in, rows_in, cols_in, count_in, feat_in,
                  own, own_cross, own_self, weight_t, spread, pair_in,
                  load_sem, y_send, y_recv, z_send, z_recv, part_send, part_recv):
    me = lax.axis_index("col")
    core = lax.rem(me, 2)
    partner = me + 1 - 2 * core
    chip = me // 2
    y, z = lax.rem(chip, n_y), chip // n_y
    loads = [
        pltpu.make_async_copy(source, target, load_sem.at[i])
        for i, (source, target) in enumerate([
            (weight_hbm, weight_in), (dst_hbm, dst_in), (att_src_hbm, att_src_in), (att_dst_hbm, att_dst_in),
            (rows_hbm, rows_in), (cols_hbm, cols_in), (count_hbm, count_in), (feat_hbm, feat_in)])
    ]
    for load in loads:
        load.start()
    barrier = pltpu.get_barrier_semaphore()

    mesh_id = pl.DeviceIdType.MESH

    def at(z_at, y_at):
        return {"col": (z_at * n_y + y_at) * 2 + core}

    y_peers = [at(z, lax.rem(y + step, n_y)) for step in range(1, n_y)]
    z_peers = [at(lax.rem(z + step, n_z), y) for step in range(1, n_z)]
    for peer in [{"col": partner}] + y_peers + z_peers:
        pl.semaphore_signal(barrier, inc=1, device_id=peer, device_id_type=mesh_id)
    for load in loads[:-1]:
        load.wait()

    weight_t[...] = jnp.transpose(weight_in[...])
    column = attention_column(att_src_in[...])
    features = dst_in[...]
    both = jnp.concatenate([features, features], axis=0)
    side = lax.broadcasted_iota(jnp.int32, both.shape, 0) // features.shape[0]
    both = jnp.where(side == core, both, jnp.zeros_like(both))
    values = project_rows_t(weight_t[...], both)
    wide = values.astype(f32)
    own[...] = jnp.concatenate(head_rows(wide, attention_column(att_dst_in[...])), axis=0)
    own_cross[...] = jnp.concatenate(head_rows(wide, column), axis=0)
    own_self[...] = values
    spread[...] = column
    cross_ref[0] = own_cross[...]
    self_ref[0] = own_self[pl.ds(pl.multiple_of(core * HALF, HALF), HALF), :]

    pl.semaphore_wait(barrier, 1 + len(y_peers) + len(z_peers))
    pair_copy = pltpu.make_async_remote_copy(
        src_ref=own, dst_ref=pair_in, send_sem=part_send.at[2], recv_sem=part_recv.at[2],
        device_id={"col": partner}, device_id_type=mesh_id)
    pair_copy.start()
    self_copy = pltpu.make_async_remote_copy(
        src_ref=own_self.at[pl.ds(pl.multiple_of((1 - core) * HALF, HALF), HALF), :], dst_ref=self_ref.at[1],
        send_sem=part_send.at[0], recv_sem=part_recv.at[0],
        device_id={"col": partner}, device_id_type=mesh_id)
    cross_copy = pltpu.make_async_remote_copy(
        src_ref=own_cross, dst_ref=cross_ref.at[1], send_sem=part_send.at[1], recv_sem=part_recv.at[1],
        device_id={"col": partner}, device_id_type=mesh_id)
    self_copy.start()
    cross_copy.start()

    loads[-1].wait()
    n_cols = scaled.shape[0]
    wide_block = 4 * TILE

    def source_block(step, carry):
        low, high = carry
        at = pl.multiple_of(step * wide_block, wide_block)
        values = project_rows_t(weight_t[...], feat_in[pl.ds(at, wide_block), :]).astype(f32)
        pad = jnp.zeros((14, TILE), f32)
        for part in range(4):
            block = 4 * step + part
            here = values[:, part * TILE : (part + 1) * TILE]
            rows = head_rows(here, spread[...])
            for h in range(HEADS):
                grow = jnp.exp(rows[h])
                fall = jnp.exp(-0.8 * rows[h])
                grow_high = grow.astype(bf16).astype(f32)
                scaled[block, h, 0:HEAD_DIM, :] = (here[h * HEAD_DIM : (h + 1) * HEAD_DIM] * grow).astype(bf16)
                scaled[block, h, HEAD_DIM:AUG, :] = jnp.concatenate(
                    [grow_high, grow - grow_high, pad], axis=0).astype(bf16)
                ratio[block, h] = jnp.broadcast_to(fall, (16, TILE)).astype(bf16)
            stacked = jnp.concatenate(rows, axis=0)
            src_score[block] = stacked
            low, high = jnp.minimum(low, stacked), jnp.maximum(high, stacked)
        return low, high

    def exchange(peers, rows, send_sem, recv_sem):
        copies = [
            pltpu.make_async_remote_copy(
                src_ref=score_ref.at[rows], dst_ref=score_ref.at[rows], send_sem=send_sem.at[i],
                recv_sem=recv_sem.at[i], device_id=peer, device_id_type=mesh_id)
            for i, peer in enumerate(peers)
        ]
        for copy in copies:
            copy.start()
        return copies

    steps = n_cols // 4
    cuts = (0, steps // 4, (5 * steps) // 8, steps)
    span = (jnp.full((HEADS, TILE), 1e30, f32), jnp.full((HEADS, TILE), -1e30, f32))
    span = lax.fori_loop(cuts[0], cuts[1], source_block, span)
    pair_copy.wait()
    score_ref[chip] = own[...] + pair_in[...]
    y_copies = exchange(y_peers, pl.ds(chip, 1), y_send, y_recv)
    span = lax.fori_loop(cuts[1], cuts[2], source_block, span)
    for copy in y_copies:
        copy.wait()
    z_copies = exchange(z_peers, pl.ds(z * n_y, n_y), z_send, z_recv)
    low, high = lax.fori_loop(cuts[2], cuts[3], source_block, span)
    range_ref[0] = low
    range_ref[1] = high

    slots = rows_in.shape[1]
    row_block = rows_in[...].astype(f32)
    slot = lax.broadcasted_iota(jnp.int32, (1, slots), 1)
    row_block = jnp.where(slot < count_in[...], row_block, 255.0)
    pad = jnp.full((1, ORDER - slots), 255.0, f32)
    row_block = jnp.concatenate([row_block, pad], axis=1)
    across = jnp.broadcast_to(row_block, (ORDER, ORDER))
    down = jnp.transpose(across)
    lane = lax.broadcasted_iota(jnp.int32, (ORDER, ORDER), 1)
    sub = lax.broadcasted_iota(jnp.int32, (ORDER, ORDER), 0)
    before = jnp.sum(jnp.where((down == across) & (sub < lane), 1.0, 0.0), axis=0, keepdims=True)
    block_id = lax.broadcasted_iota(jnp.int32, (16, ORDER), 0).astype(f32)
    counts = jnp.sum(jnp.where(block_id == row_block, 1.0, 0.0), axis=1, keepdims=True)
    pairs = jnp.floor((counts + 1.0) * 0.5)
    start = jnp.sum(jnp.where(block_id < row_block, pairs, 0.0), axis=0, keepdims=True)
    place = jnp.where(row_block < 254.0, 2.0 * start + before, -1.0)
    place_down = jnp.transpose(jnp.broadcast_to(place, (ORDER, ORDER)))
    columns = jnp.concatenate([cols_in[...].astype(f32), jnp.zeros((1, ORDER - slots), f32)], axis=1)
    lane_row = lax.broadcasted_iota(jnp.int32, (1, ORDER), 1).astype(f32)
    code = 1.0 + lane_row + 256.0 * columns + 8192.0 * jnp.minimum(row_block, 15.0)
    code_down = jnp.transpose(jnp.broadcast_to(code, (ORDER, ORDER)))
    found = jnp.sum(jnp.where(place_down == lane.astype(f32), code_down, 0.0), axis=0, keepdims=True)
    order_ref[...] = found.astype(jnp.int32)
    pairs_ref[...] = jnp.broadcast_to(jnp.sum(pairs, axis=0, keepdims=True), (1, 128)).astype(jnp.int32)

    for copy in z_copies:
        copy.wait()
    self_copy.wait()
    cross_copy.wait()


def edges_kernel(order_ref, pairs_ref, score_ref, scaled, ratio, src_score, range_ref, feat_hbm, weight_hbm, mask_hbm,
                 out_ref, ratio_dst, dst_score, acc, masks, feat_in, weight_in, mask_sem, load_sem):
    n_blocks = acc.shape[0]
    total = pairs_ref[0, 0]
    groups = (total + GROUP - 1) // GROUP

    def decode(position):
        code = order_ref[0, position]
        index = jnp.maximum(code - 1, 0)
        return code, index & 255, (index >> 8) & 31, index >> 13

    def fetch(pair):
        ring = lax.rem(pair, RING)
        for side in range(2):
            slot = decode(2 * pair + side)[1]
            pltpu.make_async_copy(mask_hbm.at[slot], masks.at[ring, side], mask_sem.at[ring]).start()

    def arrive(pair):
        ring = lax.rem(pair, RING)
        pltpu.make_async_copy(mask_hbm.at[pl.ds(0, 2)], masks.at[ring], mask_sem.at[ring]).wait()

    def mask_of(ring, side, code):
        return masks[ring, side].astype(f32) * jnp.minimum(code, 1).astype(f32)

    def prefetch(pair, carry):
        fetch(pair)
        return carry

    lax.fori_loop(0, jnp.minimum(groups * GROUP, RING - GROUP), prefetch, 0)

    spread_head = lax.broadcasted_iota(jnp.int32, (HEADS, HEADS * TILE), 0)
    spread_lane = lax.broadcasted_iota(jnp.int32, (HEADS, HEADS * TILE), 1) // TILE
    spread = jnp.where(spread_head == spread_lane, 1.0, 0.0).astype(bf16)

    def dst_block(step, carry):
        low, high = carry
        for part in range(4):
            block = 4 * step + part
            score = score_ref[block]
            dst_score[block] = score
            fall = jnp.exp(-0.8 * score).astype(bf16)
            wide = transposed_dot(fall, spread).astype(bf16)
            for h in range(HEADS):
                ratio_dst[block, h] = wide[:, h * TILE : (h + 1) * TILE]
            acc[block] = jnp.zeros(acc.shape[1:], f32)
            low, high = jnp.minimum(low, score), jnp.maximum(high, score)
        return low, high

    low, high = lax.fori_loop(0, n_blocks // 4, dst_block, (range_ref[0], range_ref[1]))
    factored = (jnp.max(high) <= SPAN) & (jnp.min(low) >= -SPAN)

    def next_group(group):
        @pl.when((group + 1) * GROUP + RING - 2 * GROUP < groups * GROUP)
        def _():
            for step in range(GROUP):
                fetch(group * GROUP + step + RING - GROUP)

        for step in range(GROUP):
            arrive(group * GROUP + step)

    @pl.when(factored)
    def _():
        def group_step(group, carry):
            next_group(group)
            one = jnp.ones((), bf16)
            for step in range(GROUP):
                pair = group * GROUP + step
                code_a, _, col_a, block = decode(2 * pair)
                code_b, _, col_b, _ = decode(2 * pair + 1)
                ring = lax.rem(pair, RING)
                mask_a = mask_of(ring, 0, code_a).astype(bf16).reshape(8, 16, TILE)
                mask_b = mask_of(ring, 1, code_b).astype(bf16).reshape(8, 16, TILE)
                for h in range(HEADS):
                    fall_dst = ratio_dst[block, h].reshape(8, 16, TILE)
                    weight_a = jnp.maximum(fall_dst * ratio[col_a, h][None], one) * mask_a
                    weight_b = jnp.maximum(fall_dst * ratio[col_b, h][None], one) * mask_b
                    edge = jnp.concatenate([weight_a.reshape(TILE, TILE), weight_b.reshape(TILE, TILE)], axis=1)
                    source = jnp.concatenate([scaled[col_a, h], scaled[col_b, h]], axis=1)
                    acc[block, h] += lax.dot_general(source, edge, (((1,), (1,)), ((), ())),
                                                     preferred_element_type=f32)
            return carry

        lax.fori_loop(0, groups, group_step, 0)

        def reference_rows(block, carry):
            for h in range(HEADS):
                acc[block, h, 66:67, :] = dst_score[block, h : h + 1, :]
            return carry

        lax.fori_loop(0, n_blocks, reference_rows, 0)

    @pl.when(jnp.logical_not(factored))
    def _():
        loads = [pltpu.make_async_copy(feat_hbm, feat_in, load_sem.at[0]),
                 pltpu.make_async_copy(weight_hbm, weight_in, load_sem.at[1])]
        for load in loads:
            load.start()
        for load in loads:
            load.wait()

        def empty_rows(block, carry):
            for h in range(HEADS):
                acc[block, h, 66:67, :] = jnp.full((1, TILE), NEG, f32)
            return carry

        lax.fori_loop(0, n_blocks, empty_rows, 0)

        def one_tile(ring, side, code, col, block):
            present = jnp.transpose(mask_of(ring, side, code)) > 0.0
            at = pl.multiple_of(col * TILE, TILE)
            values = project_t(weight_in[...], feat_in[pl.ds(at, TILE), :])
            for h in range(HEADS):
                source = as_column(src_score[col, h : h + 1, :], TILE)
                logit = leaky_relu(source + dst_score[block, h : h + 1, :])
                logit = jnp.where(present, logit, NEG)
                old_max = acc[block, h, 66:67, :]
                new_max = jnp.maximum(old_max, jnp.max(logit, axis=0, keepdims=True))
                prob = jnp.where(present, jnp.exp(logit - new_max), 0.0)
                keep = jnp.exp(old_max - new_max)
                message = jnp.dot(values[h * HEAD_DIM : (h + 1) * HEAD_DIM], prob.astype(bf16),
                                  preferred_element_type=f32)
                acc[block, h, 0:HEAD_DIM, :] = acc[block, h, 0:HEAD_DIM, :] * keep + message
                acc[block, h, 64:65, :] = acc[block, h, 64:65, :] * keep + jnp.sum(prob, axis=0, keepdims=True)
                acc[block, h, 66:67, :] = new_max

        def group_step(group, carry):
            next_group(group)

            def pair_step(step, inner):
                pair = group * GROUP + step
                ring = lax.rem(pair, RING)
                for side in range(2):
                    code, _, col, _ = decode(2 * pair + side)
                    one_tile(ring, side, code, col, decode(2 * pair)[3])
                return inner

            return lax.fori_loop(0, GROUP, pair_step, carry)

        lax.fori_loop(0, groups, group_step, 0)

    def store_block(step, carry):
        for part in range(4):
            block = 4 * step + part
            for half in range(2):
                logs = []
                for g in range(HALF_HEADS):
                    h = half * HALF_HEADS + g
                    denominator = acc[block, h, 64:65, :] + acc[block, h, 65:66, :]
                    some = denominator > 0.0
                    safe = jnp.where(some, denominator, 1.0)
                    out_ref[half, block, g * HEAD_DIM : (g + 1) * HEAD_DIM, :] = (
                        acc[block, h, 0:HEAD_DIM, :] * (1.0 / safe)).astype(bf16)
                    logs.append(jnp.where(some, acc[block, h, 66:67, :] + jnp.log(safe), NEG))
                out_ref[half, block, HALF:BLOCK, :] = pack_logs(jnp.concatenate(logs, axis=0))
        return carry

    lax.fori_loop(0, n_blocks // 4, store_block, 0)


def pack_logs(logs):
    high, middle, low = [part.astype(f32) for part in split3(logs)]
    return jnp.concatenate([high, middle, low, jnp.zeros_like(high)], axis=0).astype(bf16)


def unpack_logs(rows):
    wide = rows.astype(f32)
    n = HALF_HEADS
    return wide[0:n] + wide[n : 2 * n] + wide[2 * n : 3 * n]


def merge_blocks(blocks):
    logs = [unpack_logs(block[HALF:BLOCK]) for block in blocks]
    top = functools.reduce(jnp.maximum, logs)
    grow = [jnp.exp(log - top) for log in logs]
    total = functools.reduce(jnp.add, grow)
    share = [g * (1.0 / total) for g in grow]
    parts = []
    for h in range(HALF_HEADS):
        at = slice(h * HEAD_DIM, (h + 1) * HEAD_DIM)
        terms = [block[at].astype(f32) * s[h : h + 1] for block, s in zip(blocks, share)]
        parts.append(functools.reduce(jnp.add, terms).astype(bf16))
    return parts, pack_logs(top + jnp.log(total))


def store_block_parts(ref, index, merged):
    parts, logs = merged
    for h, part in enumerate(parts):
        ref[index + (slice(h * HEAD_DIM, (h + 1) * HEAD_DIM), slice(None))] = part
    ref[index + (slice(HALF, BLOCK), slice(None))] = logs


def merge_kernel(n_y, n_z, part_ref, score_ref, self_ref, cross_ref, bias_hbm, out_ref,
                 pair_in, summed, y_in, z_sum, z_in, self_logit, bias_in, fin, fin_in,
                 load_sem, pair_send, pair_recv, y_send, y_recv, z_send, z_recv, fin_send, fin_recv):
    me = lax.axis_index("col")
    core = lax.rem(me, 2)
    chip = me // 2
    y = lax.rem(chip, n_y)
    z = chip // n_y
    partner = me + 1 - 2 * core

    def at(z_at, y_at):
        return {"col": (z_at * n_y + y_at) * 2 + core}

    mesh_id = pl.DeviceIdType.MESH
    barrier = pltpu.get_barrier_semaphore()
    pl.semaphore_signal(barrier, inc=1, device_id={"col": partner}, device_id_type=mesh_id)
    for step in range(1, n_y):
        pl.semaphore_signal(barrier, inc=1, device_id=at(z, lax.rem(y + step, n_y)), device_id_type=mesh_id)
    for step in range(1, n_z):
        pl.semaphore_signal(barrier, inc=1, device_id=at(lax.rem(z + step, n_z), y), device_id_type=mesh_id)

    def z_of(step):
        return lax.rem(z + 1 + step, n_z)

    def pair_copy(step):
        rows = pl.ds(z_of(step) * n_y, n_y)
        return pltpu.make_async_remote_copy(
            src_ref=part_ref.at[1 - core, rows], dst_ref=pair_in.at[rows], send_sem=pair_send.at[step],
            recv_sem=pair_recv.at[step], device_id={"col": partner}, device_id_type=mesh_id)

    def y_copy(step, dy):
        block = z_of(step) * n_y + lax.rem(y + dy, n_y)
        return pltpu.make_async_remote_copy(
            src_ref=summed.at[block], dst_ref=y_in.at[step, dy - 1], send_sem=y_send.at[step, dy - 1],
            recv_sem=y_recv.at[step, dy - 1], device_id=at(z, lax.rem(y + dy, n_y)), device_id_type=mesh_id)

    def z_copy(step):
        return pltpu.make_async_remote_copy(
            src_ref=z_sum.at[step], dst_ref=z_in.at[step], send_sem=z_send.at[step],
            recv_sem=z_recv.at[step], device_id=at(z_of(step), y), device_id_type=mesh_id)

    bias_copy = pltpu.make_async_copy(bias_hbm, bias_in, load_sem)
    bias_copy.start()
    direct = score_ref[chip]
    logit = leaky_relu(direct + (cross_ref[0] + cross_ref[1]))
    self_logit[0] = logit
    self_logit[1] = jnp.concatenate([logit[HALF_HEADS:], logit[:HALF_HEADS]], axis=0)

    pl.semaphore_wait(barrier, 1 + (n_y - 1) + (n_z - 1))
    for step in range(n_z):
        pair_copy(step).start()

    def pair_merge(step):
        pair_copy(step).wait()
        for dy in range(n_y):
            block = z_of(step) * n_y + lax.rem(y + dy, n_y)
            store_block_parts(summed, (block,), merge_blocks([part_ref[core, block], pair_in[block]]))
        for dy in range(1, n_y):
            y_copy(step, dy).start()

    def y_merge(step):
        for dy in range(1, n_y):
            y_copy(step, dy).wait()
        blocks = [summed[z_of(step) * n_y + y]] + [y_in[step, dy - 1] for dy in range(1, n_y)]
        store_block_parts(z_sum, (step,), merge_blocks(blocks))
        if step < n_z - 1:
            z_copy(step).start()

    for step in range(n_z):
        pair_merge(step)
        if step > 0:
            y_merge(step - 1)
    y_merge(n_z - 1)
    for step in range(n_z - 1):
        z_copy(step).wait()

    blocks = [z_sum[n_z - 1]] + [z_in[step] for step in range(n_z - 1)]
    logs = [unpack_logs(block[HALF:BLOCK]) for block in blocks] + [self_logit[core][0:HALF_HEADS]]
    top = functools.reduce(jnp.maximum, logs)
    grow = [jnp.exp(log - top) for log in logs]
    inverse = 1.0 / functools.reduce(jnp.add, grow)
    pieces = []
    for h in range(HALF_HEADS):
        rows = slice(h * HEAD_DIM, (h + 1) * HEAD_DIM)
        terms = [block[rows].astype(f32) * g[h : h + 1] for block, g in zip(blocks, grow)]
        mine = self_ref[0, rows, :].astype(f32) + self_ref[1, rows, :].astype(f32)
        terms.append(mine * grow[-1][h : h + 1])
        pieces.append(functools.reduce(jnp.add, terms) * inverse[h : h + 1])
    mixed = jnp.transpose(jnp.concatenate(pieces, axis=0))
    bias_copy.wait()
    bias = jnp.where(core == 0, bias_in[:, 0:HALF], bias_in[:, HALF:FEAT])
    mixed = mixed + bias
    fin[...] = jnp.where(mixed > 0, mixed, jnp.exp(jnp.minimum(mixed, 0.0)) - 1.0)
    half = out_ref.shape[0]
    final = pltpu.make_async_remote_copy(
        src_ref=fin.at[pl.ds(pl.multiple_of((1 - core) * half, half), half), :], dst_ref=fin_in,
        send_sem=fin_send, recv_sem=fin_recv, device_id={"col": partner}, device_id_type=mesh_id)
    final.start()
    mine = fin[pl.ds(pl.multiple_of(core * half, half), half), :]
    final.wait()
    theirs = fin_in[...]
    out_ref[:, 0:HALF] = jnp.where(core == 0, mine, theirs)
    out_ref[:, HALF:FEAT] = jnp.where(core == 0, theirs, mine)


VMEM = pl.BlockSpec(memory_space=pltpu.VMEM)
SMEM = pl.BlockSpec(memory_space=pltpu.SMEM)
HBM = pl.BlockSpec(memory_space=pltpu.HBM)
DMA = pltpu.SemaphoreType.DMA


MIB = 1024 * 1024


def scores_and_tables(n_y, n_z, dst_feat, weight, att_src, att_dst, tile_rows, tile_cols, tile_count, src_feat):
    own = dst_feat.shape[0]
    chip = 2 * own
    n_cols = src_feat.shape[0] // TILE
    return pl.pallas_call(
        functools.partial(scores_kernel, n_y, n_z),
        name="scores_and_tables",
        out_shape=(
            jax.ShapeDtypeStruct((n_y * n_z, HEADS, chip), f32),
            jax.ShapeDtypeStruct((2, HALF, chip), bf16),
            jax.ShapeDtypeStruct((2, HEADS, chip), f32),
            jax.ShapeDtypeStruct((1, ORDER), jnp.int32),
            jax.ShapeDtypeStruct((1, 128), jnp.int32),
            jax.ShapeDtypeStruct((n_cols, HEADS, AUG, TILE), bf16),
            jax.ShapeDtypeStruct((n_cols, HEADS, 16, TILE), bf16),
            jax.ShapeDtypeStruct((n_cols, HEADS, TILE), f32),
            jax.ShapeDtypeStruct((2, HEADS, TILE), f32),
        ),
        in_specs=[HBM] * 8,
        out_specs=(VMEM,) * 9,
        scratch_shapes=[
            pltpu.VMEM(dst_feat.shape, bf16), pltpu.VMEM(weight.shape, bf16),
            pltpu.VMEM(att_src.shape, f32), pltpu.VMEM(att_dst.shape, f32),
            pltpu.VMEM(tile_rows.shape, jnp.int32), pltpu.VMEM(tile_cols.shape, jnp.int32),
            pltpu.VMEM(tile_count.shape, jnp.int32), pltpu.VMEM(src_feat.shape, bf16),
            pltpu.VMEM((HEADS, chip), f32), pltpu.VMEM((HEADS, chip), f32), pltpu.VMEM((FEAT, chip), bf16),
            pltpu.VMEM((FEAT, weight.shape[0]), bf16), pltpu.VMEM((FEAT, TILE), f32),
            pltpu.VMEM((HEADS, chip), f32),
            DMA((8,)), DMA((n_y - 1,)), DMA((n_y - 1,)), DMA((n_z - 1,)), DMA((n_z - 1,)), DMA((3,)), DMA((3,)),
        ],
        compiler_params=pltpu.CompilerParams(collective_id=0, has_side_effects=True, vmem_limit_bytes=40 * MIB),
    )(dst_feat, weight, att_src, att_dst, tile_rows, tile_cols, tile_count, src_feat)


def edge_sums(order, pairs, scores, scaled, ratio, src_score, span, src_feat, weight, masks):
    n_blocks = scores.shape[0]
    return pl.pallas_call(
        edges_kernel,
        name="edge_sums",
        out_shape=jax.ShapeDtypeStruct((2, n_blocks, BLOCK, TILE), bf16),
        in_specs=[SMEM, SMEM] + [VMEM] * 5 + [HBM] * 3,
        out_specs=VMEM,
        scratch_shapes=[
            pltpu.VMEM((n_blocks, HEADS, TILE, TILE), bf16),
            pltpu.VMEM((n_blocks, HEADS, TILE), f32),
            pltpu.VMEM((n_blocks, HEADS, AUG, TILE), f32),
            pltpu.VMEM((RING, 2, TILE, TILE), jnp.int32),
            pltpu.VMEM(src_feat.shape, bf16),
            pltpu.VMEM(weight.shape, bf16),
            DMA((RING,)), DMA((2,)),
        ],
        compiler_params=pltpu.CompilerParams(vmem_limit_bytes=40 * MIB),
    )(order, pairs, scores, scaled, ratio, src_score, span, src_feat, weight, masks)


def merge(n_y, n_z, parts, scores, self_values, cross, bias):
    n_blocks = n_y * n_z
    own = scores.shape[2] // 2
    return pl.pallas_call(
        functools.partial(merge_kernel, n_y, n_z),
        name="merge",
        out_shape=jax.ShapeDtypeStruct((own, FEAT), f32),
        in_specs=[VMEM] * 4 + [HBM],
        out_specs=VMEM,
        scratch_shapes=[
            pltpu.VMEM((n_blocks, BLOCK, TILE), bf16),
            pltpu.VMEM((n_blocks, BLOCK, TILE), bf16),
            pltpu.VMEM((n_z, n_y - 1, BLOCK, TILE), bf16),
            pltpu.VMEM((n_z, BLOCK, TILE), bf16),
            pltpu.VMEM((n_z - 1, BLOCK, TILE), bf16),
            pltpu.VMEM((2, HEADS, TILE), f32),
            pltpu.VMEM((1, FEAT), f32),
            pltpu.VMEM((TILE, HALF), f32),
            pltpu.VMEM((own, HALF), f32),
            DMA(()), DMA((n_z,)), DMA((n_z,)), DMA((n_z, n_y - 1)), DMA((n_z, n_y - 1)),
            DMA((n_z - 1,)), DMA((n_z - 1,)), DMA(()), DMA(()),
        ],
        compiler_params=pltpu.CompilerParams(collective_id=1, has_side_effects=True, vmem_limit_bytes=40 * MIB),
    )(parts, scores, self_values, cross, bias)


def local(n_col, src_feat, dst_feat, weight, att_src, att_dst, bias, tile_rows, tile_cols, tile_masks, tile_count):
    n_y = 4
    n_z = n_col // (2 * n_y)
    slots = tile_rows.shape[2]
    tile_rows, tile_cols, bias = tile_rows.reshape(1, slots), tile_cols.reshape(1, slots), bias.reshape(1, FEAT)
    tile_masks = tile_masks.reshape(slots, TILE, TILE)
    (src_feat, dst_feat, weight, att_src, att_dst, bias, tile_rows, tile_cols, tile_masks) = [
        pltpu.with_memory_space_constraint(array, pltpu.HBM)
        for array in (src_feat, dst_feat, weight, att_src, att_dst, bias, tile_rows, tile_cols, tile_masks)
    ]
    scores, self_values, cross, order, pairs, scaled, ratio, src_score, span = scores_and_tables(
        n_y, n_z, dst_feat, weight, att_src, att_dst, tile_rows, tile_cols, tile_count, src_feat)
    parts = edge_sums(order, pairs, scores, scaled, ratio, src_score, span, src_feat, weight, tile_masks)
    return merge(n_y, n_z, parts, scores, self_values, cross, bias)


def solution(mesh):
    placed = (
        P("col", None),
        P(("row", "col"), None),
        P(),
        P(),
        P(),
        P(),
        P("row", "col", None),
        P("row", "col", None),
        P("row", "col", None, None, None),
        P("row", "col"),
    )
    return jax.shard_map(
        functools.partial(local, mesh.shape["col"]), mesh=mesh, in_specs=placed,
        out_specs=P(("row", "col"), None), check_vma=False,
    )
```

```python
import functools

import jax
import jax.numpy as jnp
from jax import lax
from jax.experimental import pallas as pl
from jax.experimental.pallas import tpu as pltpu
from jax.sharding import PartitionSpec as P

HEADS = 8
HEAD_DIM = 64
TILE = 128
FEAT = HEADS * HEAD_DIM
NEG = -1e30
SPAN = 50.0
HALF = FEAT // 2
HALF_HEADS = HEADS // 2
BLOCK = HALF + 16
AUG = HEAD_DIM + 16
GROUP = 8
RING = 32
ORDER = 256

f32 = jnp.float32
bf16 = jnp.bfloat16


def leaky_relu(values):
    return jnp.maximum(values, 0.2 * values)


def split3(values):
    high = values.astype(bf16)
    rest = values - high.astype(f32)
    middle = rest.astype(bf16)
    low = (rest - middle.astype(f32)).astype(bf16)
    return high, middle, low


def transposed_dot(left, right):
    return lax.dot_general(left, right, (((0,), (0,)), ((), ())), preferred_element_type=f32)


def project_t(weight, features):
    return lax.dot_general(weight, features, (((0,), (1,)), ((), ())), preferred_element_type=f32).astype(bf16)


def project_rows_t(weight_t, features):
    return lax.dot_general(weight_t, features, (((1,), (1,)), ((), ())), preferred_element_type=f32).astype(bf16)


def attention_column(attention):
    wide = jnp.concatenate([attention] * HEADS, axis=1)
    head = lax.broadcasted_iota(jnp.int32, wide.shape, 0)
    lane_head = lax.broadcasted_iota(jnp.int32, wide.shape, 1) // HEAD_DIM
    wide = jnp.where(head == lane_head, wide, 0.0)
    terms = jnp.concatenate([part.astype(f32) for part in split3(wide)], axis=0).astype(bf16)
    return transposed_dot(terms, jnp.ones((terms.shape[0], 128), bf16))


def head_rows(values, column):
    product = values * column
    return [
        jnp.sum(product[h * HEAD_DIM : (h + 1) * HEAD_DIM], axis=0, keepdims=True) for h in range(HEADS)
    ]


def as_column(row, rows):
    return jnp.transpose(jnp.broadcast_to(row, (rows, row.shape[1])))


def scores_kernel(n_y, n_z, dst_hbm, weight_hbm, att_src_hbm, att_dst_hbm, rows_hbm, cols_hbm, count_hbm, feat_hbm,
                  score_ref, self_ref, cross_ref, order_ref, pairs_ref, scaled, ratio, src_score, range_ref,
                  dst_in, weight_in, att_src_in, att_dst_in, rows_in, cols_in, count_in, feat_in,
                  own, own_cross, own_self, weight_t, spread, pair_in,
                  load_sem, y_send, y_recv, z_send, z_recv, part_send, part_recv):
    me = lax.axis_index("col")
    core = lax.rem(me, 2)
    partner = me + 1 - 2 * core
    chip = me // 2
    y, z = lax.rem(chip, n_y), chip // n_y
    loads = [
        pltpu.make_async_copy(source, target, load_sem.at[i])
        for i, (source, target) in enumerate([
            (weight_hbm, weight_in), (dst_hbm, dst_in), (att_src_hbm, att_src_in), (att_dst_hbm, att_dst_in),
            (rows_hbm, rows_in), (cols_hbm, cols_in), (count_hbm, count_in), (feat_hbm, feat_in)])
    ]
    for load in loads:
        load.start()
    barrier = pltpu.get_barrier_semaphore()

    mesh_id = pl.DeviceIdType.MESH

    def at(z_at, y_at):
        return {"col": (z_at * n_y + y_at) * 2 + core}

    y_peers = [at(z, lax.rem(y + step, n_y)) for step in range(1, n_y)]
    z_peers = [at(lax.rem(z + step, n_z), y) for step in range(1, n_z)]
    for peer in [{"col": partner}] + y_peers + z_peers:
        pl.semaphore_signal(barrier, inc=1, device_id=peer, device_id_type=mesh_id)
    for load in loads[:-1]:
        load.wait()

    weight_t[...] = jnp.transpose(weight_in[...])
    column = attention_column(att_src_in[...])
    features = dst_in[...]
    both = jnp.concatenate([features, features], axis=0)
    side = lax.broadcasted_iota(jnp.int32, both.shape, 0) // features.shape[0]
    both = jnp.where(side == core, both, jnp.zeros_like(both))
    values = project_rows_t(weight_t[...], both)
    wide = values.astype(f32)
    own[...] = jnp.concatenate(head_rows(wide, attention_column(att_dst_in[...])), axis=0)
    own_cross[...] = jnp.concatenate(head_rows(wide, column), axis=0)
    own_self[...] = values
    spread[...] = column
    cross_ref[0] = own_cross[...]
    self_ref[0] = own_self[pl.ds(pl.multiple_of(core * HALF, HALF), HALF), :]

    pl.semaphore_wait(barrier, 1 + len(y_peers) + len(z_peers))
    pair_copy = pltpu.make_async_remote_copy(
        src_ref=own, dst_ref=pair_in, send_sem=part_send.at[2], recv_sem=part_recv.at[2],
        device_id={"col": partner}, device_id_type=mesh_id)
    pair_copy.start()
    self_copy = pltpu.make_async_remote_copy(
        src_ref=own_self.at[pl.ds(pl.multiple_of((1 - core) * HALF, HALF), HALF), :], dst_ref=self_ref.at[1],
        send_sem=part_send.at[0], recv_sem=part_recv.at[0],
        device_id={"col": partner}, device_id_type=mesh_id)
    cross_copy = pltpu.make_async_remote_copy(
        src_ref=own_cross, dst_ref=cross_ref.at[1], send_sem=part_send.at[1], recv_sem=part_recv.at[1],
        device_id={"col": partner}, device_id_type=mesh_id)
    self_copy.start()
    cross_copy.start()

    loads[-1].wait()
    n_cols = scaled.shape[0]
    wide_block = 4 * TILE

    def source_block(step, carry):
        low, high = carry
        at = pl.multiple_of(step * wide_block, wide_block)
        values = project_rows_t(weight_t[...], feat_in[pl.ds(at, wide_block), :]).astype(f32)
        pad = jnp.zeros((14, TILE), f32)
        for part in range(4):
            block = 4 * step + part
            here = values[:, part * TILE : (part + 1) * TILE]
            rows = head_rows(here, spread[...])
            for h in range(HEADS):
                grow = jnp.exp(rows[h])
                fall = jnp.exp(-0.8 * rows[h])
                grow_high = grow.astype(bf16).astype(f32)
                scaled[block, h, 0:HEAD_DIM, :] = (here[h * HEAD_DIM : (h + 1) * HEAD_DIM] * grow).astype(bf16)
                scaled[block, h, HEAD_DIM:AUG, :] = jnp.concatenate(
                    [grow_high, grow - grow_high, pad], axis=0).astype(bf16)
                ratio[block, h] = jnp.broadcast_to(fall, (16, TILE)).astype(bf16)
            stacked = jnp.concatenate(rows, axis=0)
            src_score[block] = stacked
            low, high = jnp.minimum(low, stacked), jnp.maximum(high, stacked)
        return low, high

    def exchange(peers, rows, send_sem, recv_sem):
        copies = [
            pltpu.make_async_remote_copy(
                src_ref=score_ref.at[rows], dst_ref=score_ref.at[rows], send_sem=send_sem.at[i],
                recv_sem=recv_sem.at[i], device_id=peer, device_id_type=mesh_id)
            for i, peer in enumerate(peers)
        ]
        for copy in copies:
            copy.start()
        return copies

    steps = n_cols // 4
    cuts = (0, steps // 4, (5 * steps) // 8, steps)
    span = (jnp.full((HEADS, TILE), 1e30, f32), jnp.full((HEADS, TILE), -1e30, f32))
    span = lax.fori_loop(cuts[0], cuts[1], source_block, span)
    pair_copy.wait()
    score_ref[chip] = own[...] + pair_in[...]
    y_copies = exchange(y_peers, pl.ds(chip, 1), y_send, y_recv)
    span = lax.fori_loop(cuts[1], cuts[2], source_block, span)
    for copy in y_copies:
        copy.wait()
    z_copies = exchange(z_peers, pl.ds(z * n_y, n_y), z_send, z_recv)
    low, high = lax.fori_loop(cuts[2], cuts[3], source_block, span)
    range_ref[0] = low
    range_ref[1] = high

    slots = rows_in.shape[1]
    row_block = rows_in[...].astype(f32)
    slot = lax.broadcasted_iota(jnp.int32, (1, slots), 1)
    row_block = jnp.where(slot < count_in[...], row_block, 255.0)
    pad = jnp.full((1, ORDER - slots), 255.0, f32)
    row_block = jnp.concatenate([row_block, pad], axis=1)
    across = jnp.broadcast_to(row_block, (ORDER, ORDER))
    down = jnp.transpose(across)
    lane = lax.broadcasted_iota(jnp.int32, (ORDER, ORDER), 1)
    sub = lax.broadcasted_iota(jnp.int32, (ORDER, ORDER), 0)
    before = jnp.sum(jnp.where((down == across) & (sub < lane), 1.0, 0.0), axis=0, keepdims=True)
    block_id = lax.broadcasted_iota(jnp.int32, (16, ORDER), 0).astype(f32)
    counts = jnp.sum(jnp.where(block_id == row_block, 1.0, 0.0), axis=1, keepdims=True)
    pairs = jnp.floor((counts + 1.0) * 0.5)
    start = jnp.sum(jnp.where(block_id < row_block, pairs, 0.0), axis=0, keepdims=True)
    place = jnp.where(row_block < 254.0, 2.0 * start + before, -1.0)
    place_down = jnp.transpose(jnp.broadcast_to(place, (ORDER, ORDER)))
    columns = jnp.concatenate([cols_in[...].astype(f32), jnp.zeros((1, ORDER - slots), f32)], axis=1)
    lane_row = lax.broadcasted_iota(jnp.int32, (1, ORDER), 1).astype(f32)
    code = 1.0 + lane_row + 256.0 * columns + 8192.0 * jnp.minimum(row_block, 15.0)
    code_down = jnp.transpose(jnp.broadcast_to(code, (ORDER, ORDER)))
    found = jnp.sum(jnp.where(place_down == lane.astype(f32), code_down, 0.0), axis=0, keepdims=True)
    order_ref[...] = found.astype(jnp.int32)
    pairs_ref[...] = jnp.broadcast_to(jnp.sum(pairs, axis=0, keepdims=True), (1, 128)).astype(jnp.int32)

    for copy in z_copies:
        copy.wait()
    self_copy.wait()
    cross_copy.wait()


def edges_kernel(order_ref, pairs_ref, score_ref, scaled, ratio, src_score, range_ref, feat_hbm, weight_hbm, mask_hbm,
                 out_ref, ratio_dst, dst_score, acc, masks, feat_in, weight_in, mask_sem, load_sem):
    n_blocks = acc.shape[0]
    total = pairs_ref[0, 0]
    groups = (total + GROUP - 1) // GROUP

    def decode(position):
        code = order_ref[0, position]
        index = jnp.maximum(code - 1, 0)
        return code, index & 255, (index >> 8) & 31, index >> 13

    def fetch(pair):
        ring = lax.rem(pair, RING)
        for side in range(2):
            slot = decode(2 * pair + side)[1]
            pltpu.make_async_copy(mask_hbm.at[slot], masks.at[ring, side], mask_sem.at[ring]).start()

    def arrive(pair):
        ring = lax.rem(pair, RING)
        pltpu.make_async_copy(mask_hbm.at[pl.ds(0, 2)], masks.at[ring], mask_sem.at[ring]).wait()

    def mask_of(ring, side, code):
        return masks[ring, side].astype(f32) * jnp.minimum(code, 1).astype(f32)

    spread_head = lax.broadcasted_iota(jnp.int32, (HEADS, HEADS * TILE), 0)
    spread_lane = lax.broadcasted_iota(jnp.int32, (HEADS, HEADS * TILE), 1) // TILE
    spread = jnp.where(spread_head == spread_lane, 1.0, 0.0).astype(bf16)

    early = (RING - GROUP) // (n_blocks // 4)

    def dst_block(step, carry):
        low, high = carry
        for first in range(early):
            fetch(early * step + first)
        for part in range(4):
            block = 4 * step + part
            score = score_ref[block]
            dst_score[block] = score
            fall = jnp.exp(-0.8 * score).astype(bf16)
            wide = transposed_dot(fall, spread).astype(bf16)
            for h in range(HEADS):
                ratio_dst[block, h] = wide[:, h * TILE : (h + 1) * TILE]
            acc[block] = jnp.zeros(acc.shape[1:], f32)
            low, high = jnp.minimum(low, score), jnp.maximum(high, score)
        return low, high

    low, high = lax.fori_loop(0, n_blocks // 4, dst_block, (range_ref[0], range_ref[1]))
    factored = (jnp.max(high) <= SPAN) & (jnp.min(low) >= -SPAN)

    def next_group(group):
        @pl.when((group + 1) * GROUP + RING - 2 * GROUP < groups * GROUP)
        def _():
            for step in range(GROUP):
                fetch(group * GROUP + step + RING - GROUP)

        for step in range(GROUP):
            arrive(group * GROUP + step)

    @pl.when(factored)
    def _():
        def group_step(more, group, carry):
            for step in range(GROUP):
                arrive(group * GROUP + step)
            if more:
                for step in range(GROUP):
                    fetch(group * GROUP + step + RING - GROUP)
            one = jnp.ones((), bf16)
            for step in range(GROUP):
                pair = group * GROUP + step
                code_a, _, col_a, block = decode(2 * pair)
                code_b, _, col_b, _ = decode(2 * pair + 1)
                ring = lax.rem(pair, RING)
                mask_a = mask_of(ring, 0, code_a).astype(bf16).reshape(8, 16, TILE)
                mask_b = mask_of(ring, 1, code_b).astype(bf16).reshape(8, 16, TILE)
                for h in range(HEADS):
                    fall_dst = ratio_dst[block, h].reshape(8, 16, TILE)
                    weight_a = jnp.maximum(fall_dst * ratio[col_a, h][None], one) * mask_a
                    weight_b = jnp.maximum(fall_dst * ratio[col_b, h][None], one) * mask_b
                    edge = jnp.concatenate([weight_a.reshape(TILE, TILE), weight_b.reshape(TILE, TILE)], axis=1)
                    source = jnp.concatenate([scaled[col_a, h], scaled[col_b, h]], axis=1)
                    acc[block, h] += lax.dot_general(source, edge, (((1,), (1,)), ((), ())),
                                                     preferred_element_type=f32)
            return carry

        last = groups - (RING - GROUP) // GROUP
        lax.fori_loop(0, last, functools.partial(group_step, True), 0)
        lax.fori_loop(last, groups, functools.partial(group_step, False), 0)

        def reference_rows(block, carry):
            for h in range(HEADS):
                acc[block, h, 66:67, :] = dst_score[block, h : h + 1, :]
            return carry

        lax.fori_loop(0, n_blocks, reference_rows, 0)

    @pl.when(jnp.logical_not(factored))
    def _():
        loads = [pltpu.make_async_copy(feat_hbm, feat_in, load_sem.at[0]),
                 pltpu.make_async_copy(weight_hbm, weight_in, load_sem.at[1])]
        for load in loads:
            load.start()
        for load in loads:
            load.wait()

        def empty_rows(block, carry):
            for h in range(HEADS):
                acc[block, h, 66:67, :] = jnp.full((1, TILE), NEG, f32)
            return carry

        lax.fori_loop(0, n_blocks, empty_rows, 0)

        def one_tile(ring, side, code, col, block):
            present = jnp.transpose(mask_of(ring, side, code)) > 0.0
            at = pl.multiple_of(col * TILE, TILE)
            values = project_t(weight_in[...], feat_in[pl.ds(at, TILE), :])
            for h in range(HEADS):
                source = as_column(src_score[col, h : h + 1, :], TILE)
                logit = leaky_relu(source + dst_score[block, h : h + 1, :])
                logit = jnp.where(present, logit, NEG)
                old_max = acc[block, h, 66:67, :]
                new_max = jnp.maximum(old_max, jnp.max(logit, axis=0, keepdims=True))
                prob = jnp.where(present, jnp.exp(logit - new_max), 0.0)
                keep = jnp.exp(old_max - new_max)
                message = jnp.dot(values[h * HEAD_DIM : (h + 1) * HEAD_DIM], prob.astype(bf16),
                                  preferred_element_type=f32)
                acc[block, h, 0:HEAD_DIM, :] = acc[block, h, 0:HEAD_DIM, :] * keep + message
                acc[block, h, 64:65, :] = acc[block, h, 64:65, :] * keep + jnp.sum(prob, axis=0, keepdims=True)
                acc[block, h, 66:67, :] = new_max

        def group_step(group, carry):
            next_group(group)

            def pair_step(step, inner):
                pair = group * GROUP + step
                ring = lax.rem(pair, RING)
                for side in range(2):
                    code, _, col, _ = decode(2 * pair + side)
                    one_tile(ring, side, code, col, decode(2 * pair)[3])
                return inner

            return lax.fori_loop(0, GROUP, pair_step, carry)

        lax.fori_loop(0, groups, group_step, 0)

    def store_block(step, carry):
        for part in range(4):
            block = 4 * step + part
            for half in range(2):
                logs = []
                for g in range(HALF_HEADS):
                    h = half * HALF_HEADS + g
                    denominator = acc[block, h, 64:65, :] + acc[block, h, 65:66, :]
                    some = denominator > 0.0
                    safe = jnp.where(some, denominator, 1.0)
                    out_ref[half, block, g * HEAD_DIM : (g + 1) * HEAD_DIM, :] = (
                        acc[block, h, 0:HEAD_DIM, :] * (1.0 / safe)).astype(bf16)
                    logs.append(jnp.where(some, acc[block, h, 66:67, :] + jnp.log(safe), NEG))
                out_ref[half, block, HALF:BLOCK, :] = pack_logs(jnp.concatenate(logs, axis=0))
        return carry

    lax.fori_loop(0, n_blocks // 4, store_block, 0)


def pack_logs(logs):
    high, middle, low = [part.astype(f32) for part in split3(logs)]
    return jnp.concatenate([high, middle, low, jnp.zeros_like(high)], axis=0).astype(bf16)


def unpack_logs(rows):
    wide = rows.astype(f32)
    n = HALF_HEADS
    return wide[0:n] + wide[n : 2 * n] + wide[2 * n : 3 * n]


def merge_blocks(blocks):
    logs = [unpack_logs(block[HALF:BLOCK]) for block in blocks]
    top = functools.reduce(jnp.maximum, logs)
    grow = [jnp.exp(log - top) for log in logs]
    total = functools.reduce(jnp.add, grow)
    share = [g * (1.0 / total) for g in grow]
    parts = []
    for h in range(HALF_HEADS):
        at = slice(h * HEAD_DIM, (h + 1) * HEAD_DIM)
        terms = [block[at].astype(f32) * s[h : h + 1] for block, s in zip(blocks, share)]
        parts.append(functools.reduce(jnp.add, terms).astype(bf16))
    return parts, pack_logs(top + jnp.log(total))


def store_block_parts(ref, index, merged):
    parts, logs = merged
    for h, part in enumerate(parts):
        ref[index + (slice(h * HEAD_DIM, (h + 1) * HEAD_DIM), slice(None))] = part
    ref[index + (slice(HALF, BLOCK), slice(None))] = logs


def merge_kernel(n_y, n_z, part_ref, score_ref, self_ref, cross_ref, bias_hbm, out_ref,
                 pair_in, summed, y_in, z_sum, z_in, self_logit, bias_in, fin, fin_in,
                 load_sem, pair_send, pair_recv, y_send, y_recv, z_send, z_recv, fin_send, fin_recv):
    me = lax.axis_index("col")
    core = lax.rem(me, 2)
    chip = me // 2
    y = lax.rem(chip, n_y)
    z = chip // n_y
    partner = me + 1 - 2 * core

    def at(z_at, y_at):
        return {"col": (z_at * n_y + y_at) * 2 + core}

    mesh_id = pl.DeviceIdType.MESH
    barrier = pltpu.get_barrier_semaphore()
    pl.semaphore_signal(barrier, inc=1, device_id={"col": partner}, device_id_type=mesh_id)
    for step in range(1, n_y):
        pl.semaphore_signal(barrier, inc=1, device_id=at(z, lax.rem(y + step, n_y)), device_id_type=mesh_id)
    for step in range(1, n_z):
        pl.semaphore_signal(barrier, inc=1, device_id=at(lax.rem(z + step, n_z), y), device_id_type=mesh_id)

    def z_of(step):
        return lax.rem(z + 1 + step, n_z)

    def pair_copy(step):
        rows = pl.ds(z_of(step) * n_y, n_y)
        return pltpu.make_async_remote_copy(
            src_ref=part_ref.at[1 - core, rows], dst_ref=pair_in.at[rows], send_sem=pair_send.at[step],
            recv_sem=pair_recv.at[step], device_id={"col": partner}, device_id_type=mesh_id)

    def y_copy(step, dy):
        block = z_of(step) * n_y + lax.rem(y + dy, n_y)
        return pltpu.make_async_remote_copy(
            src_ref=summed.at[block], dst_ref=y_in.at[step, dy - 1], send_sem=y_send.at[step, dy - 1],
            recv_sem=y_recv.at[step, dy - 1], device_id=at(z, lax.rem(y + dy, n_y)), device_id_type=mesh_id)

    def z_copy(step):
        return pltpu.make_async_remote_copy(
            src_ref=z_sum.at[step], dst_ref=z_in.at[step], send_sem=z_send.at[step],
            recv_sem=z_recv.at[step], device_id=at(z_of(step), y), device_id_type=mesh_id)

    bias_copy = pltpu.make_async_copy(bias_hbm, bias_in, load_sem)
    bias_copy.start()
    direct = score_ref[chip]
    logit = leaky_relu(direct + (cross_ref[0] + cross_ref[1]))
    self_logit[0] = logit
    self_logit[1] = jnp.concatenate([logit[HALF_HEADS:], logit[:HALF_HEADS]], axis=0)

    pl.semaphore_wait(barrier, 1 + (n_y - 1) + (n_z - 1))
    for step in range(n_z):
        pair_copy(step).start()

    def pair_merge(step):
        pair_copy(step).wait()
        for dy in (2, 1, 3, 0):
            block = z_of(step) * n_y + lax.rem(y + dy, n_y)
            store_block_parts(summed, (block,), merge_blocks([part_ref[core, block], pair_in[block]]))
            if dy:
                y_copy(step, dy).start()

    def y_merge(step):
        for dy in range(1, n_y):
            y_copy(step, dy).wait()
        blocks = [summed[z_of(step) * n_y + y]] + [y_in[step, dy - 1] for dy in range(1, n_y)]
        store_block_parts(z_sum, (step,), merge_blocks(blocks))
        if step < n_z - 1:
            z_copy(step).start()

    for step in range(n_z):
        pair_merge(step)
        if step > 0:
            y_merge(step - 1)
    y_merge(n_z - 1)
    for step in range(n_z - 1):
        z_copy(step).wait()

    blocks = [z_sum[n_z - 1]] + [z_in[step] for step in range(n_z - 1)]
    logs = [unpack_logs(block[HALF:BLOCK]) for block in blocks] + [self_logit[core][0:HALF_HEADS]]
    top = functools.reduce(jnp.maximum, logs)
    grow = [jnp.exp(log - top) for log in logs]
    inverse = 1.0 / functools.reduce(jnp.add, grow)
    pieces = []
    for h in range(HALF_HEADS):
        rows = slice(h * HEAD_DIM, (h + 1) * HEAD_DIM)
        terms = [block[rows].astype(f32) * g[h : h + 1] for block, g in zip(blocks, grow)]
        mine = self_ref[0, rows, :].astype(f32) + self_ref[1, rows, :].astype(f32)
        terms.append(mine * grow[-1][h : h + 1])
        pieces.append(functools.reduce(jnp.add, terms) * inverse[h : h + 1])
    mixed = jnp.transpose(jnp.concatenate(pieces, axis=0))
    bias_copy.wait()
    bias = jnp.where(core == 0, bias_in[:, 0:HALF], bias_in[:, HALF:FEAT])
    mixed = mixed + bias
    fin[...] = jnp.where(mixed > 0, mixed, jnp.exp(jnp.minimum(mixed, 0.0)) - 1.0)
    half = out_ref.shape[0]
    final = pltpu.make_async_remote_copy(
        src_ref=fin.at[pl.ds(pl.multiple_of((1 - core) * half, half), half), :], dst_ref=fin_in,
        send_sem=fin_send, recv_sem=fin_recv, device_id={"col": partner}, device_id_type=mesh_id)
    final.start()
    mine = fin[pl.ds(pl.multiple_of(core * half, half), half), :]
    final.wait()
    theirs = fin_in[...]
    out_ref[:, 0:HALF] = jnp.where(core == 0, mine, theirs)
    out_ref[:, HALF:FEAT] = jnp.where(core == 0, theirs, mine)


VMEM = pl.BlockSpec(memory_space=pltpu.VMEM)
SMEM = pl.BlockSpec(memory_space=pltpu.SMEM)
HBM = pl.BlockSpec(memory_space=pltpu.HBM)
DMA = pltpu.SemaphoreType.DMA


MIB = 1024 * 1024


def scores_and_tables(n_y, n_z, dst_feat, weight, att_src, att_dst, tile_rows, tile_cols, tile_count, src_feat):
    own = dst_feat.shape[0]
    chip = 2 * own
    n_cols = src_feat.shape[0] // TILE
    return pl.pallas_call(
        functools.partial(scores_kernel, n_y, n_z),
        name="scores_and_tables",
        out_shape=(
            jax.ShapeDtypeStruct((n_y * n_z, HEADS, chip), f32),
            jax.ShapeDtypeStruct((2, HALF, chip), bf16),
            jax.ShapeDtypeStruct((2, HEADS, chip), f32),
            jax.ShapeDtypeStruct((1, ORDER), jnp.int32),
            jax.ShapeDtypeStruct((1, 128), jnp.int32),
            jax.ShapeDtypeStruct((n_cols, HEADS, AUG, TILE), bf16),
            jax.ShapeDtypeStruct((n_cols, HEADS, 16, TILE), bf16),
            jax.ShapeDtypeStruct((n_cols, HEADS, TILE), f32),
            jax.ShapeDtypeStruct((2, HEADS, TILE), f32),
        ),
        in_specs=[HBM] * 8,
        out_specs=(VMEM,) * 9,
        scratch_shapes=[
            pltpu.VMEM(dst_feat.shape, bf16), pltpu.VMEM(weight.shape, bf16),
            pltpu.VMEM(att_src.shape, f32), pltpu.VMEM(att_dst.shape, f32),
            pltpu.VMEM(tile_rows.shape, jnp.int32), pltpu.VMEM(tile_cols.shape, jnp.int32),
            pltpu.VMEM(tile_count.shape, jnp.int32), pltpu.VMEM(src_feat.shape, bf16),
            pltpu.VMEM((HEADS, chip), f32), pltpu.VMEM((HEADS, chip), f32), pltpu.VMEM((FEAT, chip), bf16),
            pltpu.VMEM((FEAT, weight.shape[0]), bf16), pltpu.VMEM((FEAT, TILE), f32),
            pltpu.VMEM((HEADS, chip), f32),
            DMA((8,)), DMA((n_y - 1,)), DMA((n_y - 1,)), DMA((n_z - 1,)), DMA((n_z - 1,)), DMA((3,)), DMA((3,)),
        ],
        compiler_params=pltpu.CompilerParams(collective_id=0, has_side_effects=True, vmem_limit_bytes=40 * MIB),
    )(dst_feat, weight, att_src, att_dst, tile_rows, tile_cols, tile_count, src_feat)


def edge_sums(order, pairs, scores, scaled, ratio, src_score, span, src_feat, weight, masks):
    n_blocks = scores.shape[0]
    return pl.pallas_call(
        edges_kernel,
        name="edge_sums",
        out_shape=jax.ShapeDtypeStruct((2, n_blocks, BLOCK, TILE), bf16),
        in_specs=[SMEM, SMEM] + [VMEM] * 5 + [HBM] * 3,
        out_specs=VMEM,
        scratch_shapes=[
            pltpu.VMEM((n_blocks, HEADS, TILE, TILE), bf16),
            pltpu.VMEM((n_blocks, HEADS, TILE), f32),
            pltpu.VMEM((n_blocks, HEADS, AUG, TILE), f32),
            pltpu.VMEM((RING, 2, TILE, TILE), jnp.int32),
            pltpu.VMEM(src_feat.shape, bf16),
            pltpu.VMEM(weight.shape, bf16),
            DMA((RING,)), DMA((2,)),
        ],
        compiler_params=pltpu.CompilerParams(vmem_limit_bytes=40 * MIB),
    )(order, pairs, scores, scaled, ratio, src_score, span, src_feat, weight, masks)


def merge(n_y, n_z, parts, scores, self_values, cross, bias):
    n_blocks = n_y * n_z
    own = scores.shape[2] // 2
    return pl.pallas_call(
        functools.partial(merge_kernel, n_y, n_z),
        name="merge",
        out_shape=jax.ShapeDtypeStruct((own, FEAT), f32),
        in_specs=[VMEM] * 4 + [HBM],
        out_specs=VMEM,
        scratch_shapes=[
            pltpu.VMEM((n_blocks, BLOCK, TILE), bf16),
            pltpu.VMEM((n_blocks, BLOCK, TILE), bf16),
            pltpu.VMEM((n_z, n_y - 1, BLOCK, TILE), bf16),
            pltpu.VMEM((n_z, BLOCK, TILE), bf16),
            pltpu.VMEM((n_z - 1, BLOCK, TILE), bf16),
            pltpu.VMEM((2, HEADS, TILE), f32),
            pltpu.VMEM((1, FEAT), f32),
            pltpu.VMEM((TILE, HALF), f32),
            pltpu.VMEM((own, HALF), f32),
            DMA(()), DMA((n_z,)), DMA((n_z,)), DMA((n_z, n_y - 1)), DMA((n_z, n_y - 1)),
            DMA((n_z - 1,)), DMA((n_z - 1,)), DMA(()), DMA(()),
        ],
        compiler_params=pltpu.CompilerParams(collective_id=1, has_side_effects=True, vmem_limit_bytes=40 * MIB),
    )(parts, scores, self_values, cross, bias)


def local(n_col, src_feat, dst_feat, weight, att_src, att_dst, bias, tile_rows, tile_cols, tile_masks, tile_count):
    n_y = 4
    n_z = n_col // (2 * n_y)
    slots = tile_rows.shape[2]
    tile_rows, tile_cols, bias = tile_rows.reshape(1, slots), tile_cols.reshape(1, slots), bias.reshape(1, FEAT)
    tile_masks = tile_masks.reshape(slots, TILE, TILE)
    (src_feat, dst_feat, weight, att_src, att_dst, bias, tile_rows, tile_cols, tile_masks) = [
        pltpu.with_memory_space_constraint(array, pltpu.HBM)
        for array in (src_feat, dst_feat, weight, att_src, att_dst, bias, tile_rows, tile_cols, tile_masks)
    ]
    scores, self_values, cross, order, pairs, scaled, ratio, src_score, span = scores_and_tables(
        n_y, n_z, dst_feat, weight, att_src, att_dst, tile_rows, tile_cols, tile_count, src_feat)
    parts = edge_sums(order, pairs, scores, scaled, ratio, src_score, span, src_feat, weight, tile_masks)
    return merge(n_y, n_z, parts, scores, self_values, cross, bias)


def solution(mesh):
    placed = (
        P("col", None),
        P(("row", "col"), None),
        P(),
        P(),
        P(),
        P(),
        P("row", "col", None),
        P("row", "col", None),
        P("row", "col", None, None, None),
        P("row", "col"),
    )
    return jax.shard_map(
        functools.partial(local, mesh.shape["col"]), mesh=mesh, in_specs=placed,
        out_specs=P(("row", "col"), None), check_vma=False,
    )
```
